32 devices in a mesh: cells: 8 (over z, x), rep: 4 (over y, core).
Axes of the slice: x: 2, y: 2, z: 4, core: 2. Of those that a mesh axis runs over, the one named last changes fastest.
Arguments:
- snapshots: bfloat16 [512, 4, 8192], P('cells', 'rep'), may hold values from -6 to 6
- base_field: bfloat16 [4, 8192], P('rep', 'cells'), may hold values from -6 to 6
- design: float32 [512, 64], replicated, may hold values from -0.25 to 0.25
Outputs:
- basis: bfloat16 [64, 4, 8192], P(None, 'rep', 'cells')
- factor: float32 [512, 512], replicated
The draws below stay inside these ranges and needn't reach their ends.
All inputs are finite; a program needn't handle non-finite values.
Results may differ from the reference program's by a relative error of at most 0.0085.
The reference program's roundings to bfloat16 on the way (of `anomaly` and `mixing`) count: a program that leaves them out, or rounds other values in their place, can miss the bound.
Values may be sent and summed in bfloat16 or wider, within the bound.
No kernel may reach another device: no remote copies, remote signals or barrier semaphores. Data moves between devices by JAX's collectives and lax.ppermute only.
A program may use at most 256 MiB of HBM per device.

```python
import math
import jax
import jax.numpy as jnp
from jax import lax

RUNS = 512
MODES = 64
CELL_DEV = 1024
CPR = 8192
NCELL = 32768
N_CELLS = 8
N_REP = 4


def exact_bf(values):
    return values.astype(jnp.bfloat16).astype(jnp.float32)


def draw_snapshots(key, part):
    decay_ratio = 0.75
    first_scale = 0.8
    total = jnp.zeros((RUNS, N_REP, CPR), jnp.float32)
    for mode_rank in range(12):
        mode_key = jax.random.fold_in(key, mode_rank)
        coef_key, field_key, region_key = jax.random.split(mode_key, 3)
        amplitude = first_scale * decay_ratio ** mode_rank
        weights = jax.random.truncated_normal(coef_key, -3.0, 3.0, (RUNS, 1, 1), jnp.float32) * amplitude
        region = jnp.exp(jax.random.uniform(region_key, (1, N_REP, 1), jnp.float32, math.log(0.5), math.log(2.0)))
        pattern = jax.random.truncated_normal(field_key, -3.0, 3.0, (1, N_REP, CPR), jnp.float32)
        total = total + exact_bf(weights) * exact_bf(pattern * region)
    noise_key = jax.random.fold_in(key, 7001)
    scale_key, field_key = jax.random.split(noise_key)
    noise_scale = jnp.exp(jax.random.uniform(scale_key, (RUNS, 1, 1), jnp.float32, math.log(0.3), math.log(1.0)))
    noise = jax.random.truncated_normal(field_key, -3.0, 3.0, (RUNS, N_REP, CPR), jnp.float32)
    total = total + exact_bf(noise_scale) * exact_bf(noise)
    return jnp.clip(total, -6.0, 6.0).astype(jnp.bfloat16)


def block_levels(stream_key, shape, cuts, least, high):
    def one(axis_at, parts):
        draws = jax.random.uniform(jax.random.fold_in(jax.random.fold_in(stream_key, 6), axis_at), (parts,), jnp.float32, least / len(cuts), high / len(cuts))
        return jnp.repeat(jnp.exp(draws), shape[axis_at] // parts).reshape((-1,) + (1,) * (len(shape) - axis_at - 1))

    level = one(*cuts[0])
    for cut in cuts[1:]:
        level = level * one(*cut)
    return level


def normal_values(own_key, shape, deviation, limit, cuts=(), held_as=jnp.bfloat16):
    drawn = jax.random.normal(own_key, shape, jnp.float32) * deviation
    if len(cuts) > 0:
        drawn = block_levels(own_key, shape, cuts, -0.22, 0.18) * drawn
    return jnp.clip(drawn, min=-limit, max=limit).astype(held_as)


def setup_inputs(seed: int = 0) -> dict:
    arg_keys = jax.random.split(jax.random.key(seed), 4)
    return {
        "snapshots": draw_snapshots(jax.random.fold_in(arg_keys[3], 71), 0),
        "base_field": normal_values(arg_keys[1], (N_REP, CPR), 1.0, 6.0, ((0, 4), (1, 8))),
        "design": normal_values(arg_keys[2], (RUNS, MODES), RUNS ** -0.5, 0.25, (), jnp.float32),
    }


def upper_factor(gram):
    size_all = gram.shape[0]
    width = 64
    high = lax.Precision.HIGHEST
    columns = lax.broadcasted_iota(jnp.int32, (1, size_all), 1)
    work = gram
    rows_out = []
    for block in range(size_all // width):
        start = block * width
        panel = work[start:start + width, :]
        result = jnp.zeros((width, size_all), jnp.float32)

        def step(index, carry):
            panel_now, result_now = carry
            line = lax.dynamic_index_in_dim(panel_now, index, 0, keepdims=True)
            where = columns == index + start
            pivot = jnp.sqrt(jnp.sum(jnp.where(where, line, 0.0)))
            line = jnp.where(columns >= index + start, line / pivot, 0.0)
            coeffs = line[:, start:start + width]
            panel_now = panel_now - coeffs.T * line
            result_now = lax.dynamic_update_index_in_dim(result_now, line[0], index, 0)
            return (panel_now, result_now)
        panel, result = lax.fori_loop(0, width, step, (panel, result))
        rows_out.append(result)
        work = work - jnp.dot(result.T, result, precision=high, preferred_element_type=jnp.float32)
    return jnp.concatenate(rows_out, axis=0)

def back_solve(factor, right):
    size_all = factor.shape[0]
    width = 64
    high = lax.Precision.HIGHEST
    count = size_all // width
    solved = [None] * count
    rows_small = lax.broadcasted_iota(jnp.int32, (width, 1), 0)
    for block in reversed(range(count)):
        start = block * width
        rhs = right[start:start + width, :]
        if block + 1 < count:
            later = jnp.concatenate(solved[block + 1:], axis=0)
            rhs = rhs - jnp.dot(factor[start:start + width, start + width:], later, precision=high, preferred_element_type=jnp.float32)
        square = factor[start:start + width, start:start + width]
        answer = jnp.zeros_like(rhs)

        def step(turn, answer_now):
            index = width - 1 - turn
            line = lax.dynamic_index_in_dim(square, index, 0, keepdims=True)
            target = lax.dynamic_index_in_dim(rhs, index, 0, keepdims=True)
            diag = jnp.sum(jnp.where(rows_small.T == index, line, 0.0))
            value = (target - jnp.dot(line, answer_now, precision=high, preferred_element_type=jnp.float32)) / diag
            return jnp.where(rows_small == index, value, answer_now)
        solved[block] = lax.fori_loop(0, width, step, answer)
    return jnp.concatenate(solved, axis=0)

def reference(snapshots, base_field, design):
    blocks = snapshots.reshape(RUNS, N_REP * N_CELLS, CELL_DEV).transpose(1, 0, 2)
    bases = base_field.reshape(N_REP * N_CELLS, CELL_DEV)

    def anomaly_of(block, base):
        return (block.astype(jnp.float32) - base.astype(jnp.float32)[None, :]).astype(jnp.bfloat16)

    def accumulate(total, pair):
        anomaly = anomaly_of(pair[0], pair[1])
        part = lax.dot_general(anomaly, anomaly, (((1,), (1,)), ((), ())), preferred_element_type=jnp.float32)
        return (total + part, None)
    gram, _ = lax.scan(accumulate, jnp.zeros((RUNS, RUNS), jnp.float32), (blocks, bases))
    gram = gram / NCELL
    factor = upper_factor(gram)
    mixing = back_solve(factor, design).astype(jnp.bfloat16)

    def project(pair):
        anomaly = anomaly_of(pair[0], pair[1])
        return lax.dot_general(mixing, anomaly, (((0,), (0,)), ((), ())), preferred_element_type=jnp.float32).astype(jnp.bfloat16)
    fields = lax.map(project, (blocks, bases))
    basis = fields.transpose(1, 0, 2).reshape(MODES, N_REP, CPR)
    return (basis, factor)
```

```python
import jax
import jax.numpy as jnp
from jax import lax
from jax.experimental import pallas as pl
from jax.experimental.pallas import tpu as pltpu
from jax.sharding import PartitionSpec as P

BLOCK = 128
HALF = BLOCK // 2
LANES = 128
AXES = ("cells", "rep")
HIGH = lax.Precision.HIGHEST
NARROW = (((1,), (0,)), ((), ()))
FIRST = (((0,), (0,)), ((), ()))
LAST = (((1,), (1,)), ((), ()))


def dot(a, b, dims=NARROW):
    return lax.dot_general(a, b, dims, precision=HIGH, preferred_element_type=jnp.float32)


def upper_pairs(count):
    return [(i, j) for i in range(count) for j in range(i, count)]


def factor_half(square):
    tile = (8, LANES)
    sub = lax.broadcasted_iota(jnp.int32, tile, 0)
    eye = (
        lax.broadcasted_iota(jnp.int32, (HALF, HALF), 0)
        == lax.broadcasted_iota(jnp.int32, (HALF, HALF), 1)
    ).astype(jnp.float32)
    both = jnp.concatenate([square, eye], axis=1)
    count = HALF // 8
    strips = [both[8 * j : 8 * j + 8, :] for j in range(count)]
    for m in range(count):
        spread = {}
        for j in range(m, count):
            for t in range(8):
                at = 8 * m + t
                spread[j, t] = jnp.broadcast_to(strips[j][:, at : at + 1], tile)
        for t in range(8):
            root = lax.rsqrt(jnp.broadcast_to(spread[m, t][t : t + 1, :], tile))
            inverse = root * root
            row = jnp.broadcast_to(strips[m][t : t + 1, :], tile)
            scaled = row * inverse
            later = {
                u: jnp.broadcast_to(spread[m, u][t : t + 1, :], tile) * inverse
                for u in range(t + 1, 8)
            }
            for j in range(m, count):
                column = spread[j, t]
                if j == m:
                    column = jnp.where(sub > t, column, 0.0)
                for u in range(t + 1, 8):
                    spread[j, u] = spread[j, u] - column * later[u]
                updated = strips[j] - column * scaled
                strips[j] = jnp.where(sub == t, row * root, updated) if j == m else updated
    return jnp.concatenate(strips, axis=0)


def upper_part(square):
    shape = square.shape
    keep = lax.broadcasted_iota(jnp.int32, shape, 0) <= lax.broadcasted_iota(jnp.int32, shape, 1)
    return jnp.where(keep, square, 0.0)


def factor_block(square):
    low, high = slice(0, HALF), slice(HALF, BLOCK)
    both = factor_half(square[low, low])
    r00, v00 = upper_part(both[:, :HALF]), both[:, HALF:]
    r01 = dot(v00, square[low, high])
    both = factor_half(square[high, high] - dot(r01, r01, FIRST))
    r11, v11 = upper_part(both[:, :HALF]), both[:, HALF:]
    v10 = -dot(v11, dot(r01, v00, FIRST))
    zero = jnp.zeros((HALF, HALF), jnp.float32)
    factor = jnp.concatenate(
        [jnp.concatenate([r00, r01], axis=1), jnp.concatenate([zero, r11], axis=1)], axis=0
    )
    inverse = jnp.concatenate(
        [jnp.concatenate([v00, zero], axis=1), jnp.concatenate([v10, v11], axis=1)], axis=0
    )
    return factor, inverse


def gram_kernel(panel_ref, base_ref, anomaly_ref, gram_ref):
    count = panel_ref.shape[0] // BLOCK
    anomaly_ref[...] = (
        panel_ref[...].astype(jnp.float32) - base_ref[...].astype(jnp.float32)
    ).astype(jnp.bfloat16)
    at = 0
    for i in range(count):
        rows = anomaly_ref[pl.ds(i * BLOCK, BLOCK), :]
        rest = anomaly_ref[pl.ds(i * BLOCK, (count - i) * BLOCK), :]
        part = lax.dot_general(rows, rest, LAST, preferred_element_type=jnp.float32)
        for j in range(count - i):
            gram_ref[pl.ds(at * BLOCK, BLOCK), :] = part[:, j * BLOCK : (j + 1) * BLOCK]
            at += 1


def factor_kernel(
    scale, place_ref, mine_ref, other_ref, design_ref, anomaly_ref, basis_ref, factor_ref, gram_ref, inv_ref
):
    count = factor_ref.shape[0] // BLOCK
    slots, size = mine_ref.shape[0], mine_ref.shape[1]
    half, quarter = place_ref[0], place_ref[1]
    for slot in range(slots):
        piece = lax.bitwise_xor(quarter, slot)
        for side, ref in ((half, mine_ref), (1 - half, other_ref)):
            start = pl.multiple_of((side * slots + piece) * size, 8)
            gram_ref[pl.ds(start, size), :] = ref[slot] * scale
    pairs = upper_pairs(count)
    where = {pair: at for at, pair in enumerate(pairs)}

    def gram_at(i, j):
        return pl.ds(where[i, j] * BLOCK, BLOCK)

    def span(i):
        return pl.ds(i * BLOCK, BLOCK)

    for k in range(count):
        factor, inverse = factor_block(gram_ref[gram_at(k, k), :])
        factor_ref[span(k), span(k)] = factor
        rows = {}
        for j in range(k + 1, count):
            rows[j] = dot(inverse, gram_ref[gram_at(k, j), :])
            factor_ref[span(k), span(j)] = rows[j]
            factor_ref[span(j), span(k)] = jnp.zeros((BLOCK, BLOCK), jnp.float32)
        for i in range(k + 1, count):
            for j in range(i, count):
                gram_ref[gram_at(i, j), :] = gram_ref[gram_at(i, j), :] - dot(
                    rows[i], rows[j], FIRST
                )
        done = {}
        for j in range(k):
            done[j] = dot(inverse, inv_ref[span(k), span(j)])
            inv_ref[span(k), span(j)] = done[j]
        done[k] = inverse
        inv_ref[span(k), span(k)] = inverse
        for i in range(k + 1, count):
            for j in range(k + 1):
                old = inv_ref[span(i), span(j)] if j < k else 0.0
                inv_ref[span(i), span(j)] = old - dot(rows[i], done[j], FIRST)
    columns = []
    for j in range(count):
        tail = pl.ds(j * BLOCK, (count - j) * BLOCK)
        columns.append(dot(design_ref[tail, :], inv_ref[tail, span(j)], FIRST))
    mixing = jnp.concatenate(columns, axis=1).astype(jnp.bfloat16)
    basis_ref[...] = lax.dot_general(
        mixing, anomaly_ref[...], NARROW, preferred_element_type=jnp.float32
    ).astype(jnp.bfloat16)


def swap(value, mask, devices):
    return lax.ppermute(value, AXES, [(i, i ^ mask) for i in range(devices)])


def shards(snapshots, base_field, design):
    n_cells, n_rep = lax.axis_size("cells"), lax.axis_size("rep")
    devices = n_cells * n_rep
    local_runs = snapshots.shape[0]
    runs, modes = design.shape
    slab = base_field.shape[1]
    blocks = runs // BLOCK
    packed = len(upper_pairs(blocks)) * BLOCK
    slabs = snapshots.reshape(local_runs, n_cells, slab).transpose(1, 0, 2)
    panel = lax.all_to_all(slabs, "cells", split_axis=0, concat_axis=0, tiled=True)
    vmem = pl.BlockSpec(memory_space=pltpu.VMEM)
    anomaly, gram = pl.pallas_call(
        gram_kernel,
        out_shape=(
            jax.ShapeDtypeStruct((runs, slab), jnp.bfloat16),
            jax.ShapeDtypeStruct((packed, LANES), jnp.float32),
        ),
        in_specs=[vmem, vmem],
        out_specs=(vmem, vmem),
        compiler_params=pltpu.CompilerParams(vmem_limit_bytes=32 * 2**20),
    )(panel.reshape(runs, slab), base_field)

    me = lax.axis_index("cells") * n_rep + lax.axis_index("rep")
    half, quarter = me % 2, (me // 2) % 4
    halves = gram.reshape(2, packed // 2, LANES)
    got = swap(lax.dynamic_index_in_dim(halves, 1 - half, 0, keepdims=False), 1, devices)
    own = lax.dynamic_index_in_dim(halves, half, 0, keepdims=False) + got
    quarters = own.reshape(4, packed // 8, LANES)
    total = lax.dynamic_index_in_dim(quarters, quarter, 0, keepdims=False)
    parts = [
        swap(lax.dynamic_index_in_dim(quarters, quarter ^ m, 0, keepdims=False), 2 * m, devices)
        for m in (1, 2, 3)
    ]
    for part in parts:
        total = total + part
    mask = 8
    while mask < devices:
        total = total + swap(total, mask, devices)
        mask *= 2
    mine = jnp.stack([total] + [swap(total, 2 * m, devices) for m in (1, 2, 3)])
    other = swap(mine, 1, devices)

    def kernel(*refs):
        factor_kernel(1.0 / (slab * devices), *refs)

    basis, factor = pl.pallas_call(
        kernel,
        out_shape=(
            jax.ShapeDtypeStruct((modes, slab), jnp.bfloat16),
            jax.ShapeDtypeStruct((runs, runs), jnp.float32),
        ),
        in_specs=[pl.BlockSpec(memory_space=pltpu.SMEM), vmem, vmem, vmem, vmem],
        out_specs=(vmem, vmem),
        scratch_shapes=[
            pltpu.VMEM((packed, LANES), jnp.float32),
            pltpu.VMEM((runs, runs), jnp.float32),
        ],
        compiler_params=pltpu.CompilerParams(vmem_limit_bytes=32 * 2**20),
    )(jnp.stack([half, quarter]).astype(jnp.int32), mine, other, design, anomaly)
    return (basis.reshape(modes, 1, slab), factor)


def solution(mesh):
    in_specs = (P("cells", "rep", None), P("rep", "cells"), P())
    out_specs = (P(None, "rep", "cells"), P())
    return jax.shard_map(shards, mesh=mesh, in_specs=in_specs, out_specs=out_specs, check_vma=False)
```

```python
import functools

import jax
import jax.numpy as jnp
from jax import lax
from jax.experimental import pallas as pl
from jax.experimental.pallas import tpu as pltpu
from jax.sharding import PartitionSpec as P

BLOCK = 128
HALF = BLOCK // 2
LANES = 128
AXES = ("cells", "rep")
HIGH = lax.Precision.HIGHEST
NARROW = (((1,), (0,)), ((), ()))
FIRST = (((0,), (0,)), ((), ()))
LAST = (((1,), (1,)), ((), ()))


def dot(a, b, dims=NARROW):
    return lax.dot_general(a, b, dims, precision=HIGH, preferred_element_type=jnp.float32)


def upper_pairs(count):
    return [(i, j) for i in range(count) for j in range(i, count)]


def factor_half(square):
    tile = (8, LANES)
    sub = lax.broadcasted_iota(jnp.int32, tile, 0)
    eye = (
        lax.broadcasted_iota(jnp.int32, (HALF, HALF), 0)
        == lax.broadcasted_iota(jnp.int32, (HALF, HALF), 1)
    ).astype(jnp.float32)
    both = jnp.concatenate([square, eye], axis=1)
    count = HALF // 8
    strips = [both[8 * j : 8 * j + 8, :] for j in range(count)]
    for m in range(count):
        spread = {}
        for j in range(m, count):
            for t in range(8):
                at = 8 * m + t
                spread[j, t] = jnp.broadcast_to(strips[j][:, at : at + 1], tile)
        for t in range(8):
            root = lax.rsqrt(jnp.broadcast_to(spread[m, t][t : t + 1, :], tile))
            inverse = root * root
            row = jnp.broadcast_to(strips[m][t : t + 1, :], tile)
            scaled = row * inverse
            later = {
                u: jnp.broadcast_to(spread[m, u][t : t + 1, :], tile) * inverse
                for u in range(t + 1, 8)
            }
            for j in range(m, count):
                column = spread[j, t]
                if j == m:
                    column = jnp.where(sub > t, column, 0.0)
                for u in range(t + 1, 8):
                    spread[j, u] = spread[j, u] - column * later[u]
                updated = strips[j] - column * scaled
                strips[j] = jnp.where(sub == t, row * root, updated) if j == m else updated
    return jnp.concatenate(strips, axis=0)


def upper_part(square):
    shape = square.shape
    keep = lax.broadcasted_iota(jnp.int32, shape, 0) <= lax.broadcasted_iota(jnp.int32, shape, 1)
    return jnp.where(keep, square, 0.0)


def factor_block(square):
    low, high = slice(0, HALF), slice(HALF, BLOCK)
    both = factor_half(square[low, low])
    r00, v00 = upper_part(both[:, :HALF]), both[:, HALF:]
    r01 = dot(v00, square[low, high])
    both = factor_half(square[high, high] - dot(r01, r01, FIRST))
    r11, v11 = upper_part(both[:, :HALF]), both[:, HALF:]
    v10 = -dot(v11, dot(r01, v00, FIRST))
    zero = jnp.zeros((HALF, HALF), jnp.float32)
    factor = jnp.concatenate(
        [jnp.concatenate([r00, r01], axis=1), jnp.concatenate([zero, r11], axis=1)], axis=0
    )
    inverse = jnp.concatenate(
        [jnp.concatenate([v00, zero], axis=1), jnp.concatenate([v10, v11], axis=1)], axis=0
    )
    return factor, inverse


def pack_kernel(partners, waited, place_ref, field_ref, *refs):
    piece_refs = refs[waited:]
    slab = piece_refs[0].shape[1]
    for partner, piece_ref in zip(partners, piece_refs):
        start = lax.bitwise_xor(place_ref[0], partner) * slab
        piece_ref[...] = field_ref[:, pl.ds(pl.multiple_of(start, LANES), slab)]


def gram_kernel(place_ref, *refs):
    *piece_refs, base_ref, anomaly_ref, gram_ref = refs
    count = anomaly_ref.shape[0] // BLOCK
    base = base_ref[...].astype(jnp.float32)
    for partner, piece_ref in enumerate(piece_refs):
        size = piece_ref.shape[0]
        start = lax.bitwise_xor(place_ref[0], partner) * size if len(piece_refs) > 1 else 0
        anomaly_ref[pl.ds(pl.multiple_of(start, size), size), :] = (
            piece_ref[...].astype(jnp.float32) - base
        ).astype(jnp.bfloat16)
    at = 0
    for i in range(count):
        rows = anomaly_ref[pl.ds(i * BLOCK, BLOCK), :]
        rest = anomaly_ref[pl.ds(i * BLOCK, (count - i) * BLOCK), :]
        part = lax.dot_general(rows, rest, LAST, preferred_element_type=jnp.float32)
        for j in range(count - i):
            gram_ref[pl.ds(at * BLOCK, BLOCK), :] = part[:, j * BLOCK : (j + 1) * BLOCK]
            at += 1


def factor_kernel(
    scale, place_ref, mine_ref, other_ref, design_ref, anomaly_ref, basis_ref, factor_ref, gram_ref, inv_ref
):
    count = factor_ref.shape[0] // BLOCK
    slots, size = mine_ref.shape[0], mine_ref.shape[1]
    half, quarter = place_ref[0], place_ref[1]
    for slot in range(slots):
        piece = lax.bitwise_xor(quarter, slot)
        for side, ref in ((half, mine_ref), (1 - half, other_ref)):
            start = pl.multiple_of((side * slots + piece) * size, 8)
            gram_ref[pl.ds(start, size), :] = ref[slot] * scale
    pairs = upper_pairs(count)
    where = {pair: at for at, pair in enumerate(pairs)}

    def gram_at(i, j):
        return pl.ds(where[i, j] * BLOCK, BLOCK)

    def span(i):
        return pl.ds(i * BLOCK, BLOCK)

    for k in range(count):
        factor, inverse = factor_block(gram_ref[gram_at(k, k), :])
        factor_ref[span(k), span(k)] = factor
        rows = {}
        for j in range(k + 1, count):
            rows[j] = dot(inverse, gram_ref[gram_at(k, j), :])
            factor_ref[span(k), span(j)] = rows[j]
            factor_ref[span(j), span(k)] = jnp.zeros((BLOCK, BLOCK), jnp.float32)
        for i in range(k + 1, count):
            for j in range(i, count):
                gram_ref[gram_at(i, j), :] = gram_ref[gram_at(i, j), :] - dot(
                    rows[i], rows[j], FIRST
                )
        done = {}
        for j in range(k):
            done[j] = dot(inverse, inv_ref[span(k), span(j)])
            inv_ref[span(k), span(j)] = done[j]
        done[k] = inverse
        inv_ref[span(k), span(k)] = inverse
        for i in range(k + 1, count):
            for j in range(k + 1):
                old = inv_ref[span(i), span(j)] if j < k else 0.0
                inv_ref[span(i), span(j)] = old - dot(rows[i], done[j], FIRST)
    columns = []
    for j in range(count):
        tail = pl.ds(j * BLOCK, (count - j) * BLOCK)
        columns.append(dot(design_ref[tail, :], inv_ref[tail, span(j)], FIRST))
    mixing = jnp.concatenate(columns, axis=1).astype(jnp.bfloat16)
    basis_ref[...] = lax.dot_general(
        mixing, anomaly_ref[...], NARROW, preferred_element_type=jnp.float32
    ).astype(jnp.bfloat16)


def swap(value, mask, devices):
    return lax.ppermute(value, AXES, [(i, i ^ mask) for i in range(devices)])


def shards(snapshots, base_field, design):
    n_cells, n_rep = lax.axis_size("cells"), lax.axis_size("rep")
    devices = n_cells * n_rep
    local_runs = snapshots.shape[0]
    runs, modes = design.shape
    slab = base_field.shape[1]
    blocks = runs // BLOCK
    packed = len(upper_pairs(blocks)) * BLOCK
    vmem = pl.BlockSpec(memory_space=pltpu.VMEM)
    smem = pl.BlockSpec(memory_space=pltpu.SMEM)
    column = lax.axis_index("cells").astype(jnp.int32).reshape(1)
    if n_cells == 8 and local_runs % 16 == 0:
        field = snapshots.reshape(local_runs, n_cells * slab)
        pieces = {}
        for partners, after in (((4, 5, 3, 0), ()), ((6, 7, 2, 1), (3,))):
            packed_pieces = pl.pallas_call(
                functools.partial(pack_kernel, partners, len(after)),
                out_shape=[jax.ShapeDtypeStruct((local_runs, slab), jnp.bfloat16)] * len(partners),
                in_specs=[smem, vmem] + [pl.BlockSpec(memory_space=pl.ANY)] * len(after),
                out_specs=[vmem] * len(partners),
                compiler_params=pltpu.CompilerParams(vmem_limit_bytes=16 * 2**20),
            )(column, field, *[pieces[m] for m in after])
            for m, piece in zip(partners, packed_pieces):
                route = [(i, i ^ m) for i in range(n_cells)]
                pieces[m] = lax.ppermute(piece, "cells", route) if m else piece
        panel = [pieces[m] for m in range(n_cells)]
    else:
        slabs = snapshots.reshape(local_runs, n_cells, slab).transpose(1, 0, 2)
        moved = lax.all_to_all(slabs, "cells", split_axis=0, concat_axis=0, tiled=True)
        panel = [moved.reshape(runs, slab)]
    anomaly, gram = pl.pallas_call(
        gram_kernel,
        out_shape=(
            jax.ShapeDtypeStruct((runs, slab), jnp.bfloat16),
            jax.ShapeDtypeStruct((packed, LANES), jnp.float32),
        ),
        in_specs=[smem] + [vmem] * (len(panel) + 1),
        out_specs=(vmem, vmem),
        compiler_params=pltpu.CompilerParams(vmem_limit_bytes=32 * 2**20),
    )(column, *panel, base_field)

    me = lax.axis_index("cells") * n_rep + lax.axis_index("rep")
    half, quarter = me % 2, (me // 2) % 4
    halves = gram.reshape(2, packed // 2, LANES)
    got = swap(lax.dynamic_index_in_dim(halves, 1 - half, 0, keepdims=False), 1, devices)
    own = lax.dynamic_index_in_dim(halves, half, 0, keepdims=False) + got
    quarters = own.reshape(4, packed // 8, LANES)
    total = lax.dynamic_index_in_dim(quarters, quarter, 0, keepdims=False)
    parts = [
        swap(lax.dynamic_index_in_dim(quarters, quarter ^ m, 0, keepdims=False), 2 * m, devices)
        for m in (1, 2, 3)
    ]
    for part in parts:
        total = total + part
    mask = 8
    while mask < devices:
        total = total + swap(total, mask, devices)
        mask *= 2
    mine = jnp.stack([total] + [swap(total, 2 * m, devices) for m in (1, 2, 3)])
    other = swap(mine, 1, devices)

    def kernel(*refs):
        factor_kernel(1.0 / (slab * devices), *refs)

    basis, factor = pl.pallas_call(
        kernel,
        out_shape=(
            jax.ShapeDtypeStruct((modes, slab), jnp.bfloat16),
            jax.ShapeDtypeStruct((runs, runs), jnp.float32),
        ),
        in_specs=[smem, vmem, vmem, vmem, vmem],
        out_specs=(vmem, vmem),
        scratch_shapes=[
            pltpu.VMEM((packed, LANES), jnp.float32),
            pltpu.VMEM((runs, runs), jnp.float32),
        ],
        compiler_params=pltpu.CompilerParams(vmem_limit_bytes=32 * 2**20),
    )(jnp.stack([half, quarter]).astype(jnp.int32), mine, other, design, anomaly)
    return (basis.reshape(modes, 1, slab), factor)


def solution(mesh):
    in_specs = (P("cells", "rep", None), P("rep", "cells"), P())
    out_specs = (P(None, "rep", "cells"), P())
    return jax.shard_map(shards, mesh=mesh, in_specs=in_specs, out_specs=out_specs, check_vma=False)
```

```python
import functools

import jax
import jax.numpy as jnp
from jax import lax
from jax.experimental import pallas as pl
from jax.experimental.pallas import tpu as pltpu
from jax.sharding import PartitionSpec as P

BLOCK = 128
HALF = BLOCK // 2
LANES = 128
AXES = ("cells", "rep")
HIGH = lax.Precision.HIGHEST
NARROW = (((1,), (0,)), ((), ()))
FIRST = (((0,), (0,)), ((), ()))
LAST = (((1,), (1,)), ((), ()))


def dot(a, b, dims=NARROW):
    return lax.dot_general(a, b, dims, precision=HIGH, preferred_element_type=jnp.float32)


def upper_pairs(count):
    return [(i, j) for i in range(count) for j in range(i, count)]


def factor_half(square):
    tile = (8, LANES)
    sub = lax.broadcasted_iota(jnp.int32, tile, 0)
    eye = (
        lax.broadcasted_iota(jnp.int32, (HALF, HALF), 0)
        == lax.broadcasted_iota(jnp.int32, (HALF, HALF), 1)
    ).astype(jnp.float32)
    both = jnp.concatenate([square, eye], axis=1)
    count = HALF // 8
    strips = [both[8 * j : 8 * j + 8, :] for j in range(count)]

    def spread_row(value, at):
        return jnp.broadcast_to(value[at : at + 1, :], tile)

    def spread_column(value, at):
        return jnp.broadcast_to(value[:, at : at + 1], tile)

    ahead = [spread_column(strips[0], t) for t in range(8)]
    for m in range(count):
        columns = {(m, t): ahead[t] for t in range(8)}
        for j in range(m + 1, count):
            for t in range(8):
                columns[j, t] = spread_column(strips[j], 8 * m + t)
        if m + 1 < count:
            ahead = [spread_column(strips[m + 1], 8 * m + 8 + t) for t in range(8)]
        corner = {(t, u): spread_row(columns[m, u], t) for t in range(8) for u in range(t, 8)}
        for t in range(8):
            root = lax.rsqrt(corner[t, t])
            line = {u: corner[t, u] * root for u in range(t + 1, 8)}
            for u in range(t + 1, 8):
                for v in range(u, 8):
                    corner[u, v] = corner[u, v] - line[u] * line[v]
            row = spread_row(strips[m], t) * root
            for j in range(m, count):
                column = columns[j, t] * root
                if j == m:
                    column = jnp.where(sub > t, column, 0.0)
                for u in range(t + 1, 8):
                    columns[j, u] = columns[j, u] - column * line[u]
                updated = strips[j] - column * row
                strips[j] = jnp.where(sub == t, row, updated) if j == m else updated
                if j == m + 1:
                    ahead = [ahead[u] - column * spread_row(column, u) for u in range(8)]
    return jnp.concatenate(strips, axis=0)


def upper_part(square):
    shape = square.shape
    keep = lax.broadcasted_iota(jnp.int32, shape, 0) <= lax.broadcasted_iota(jnp.int32, shape, 1)
    return jnp.where(keep, square, 0.0)


def factor_block(square):
    low, high = slice(0, HALF), slice(HALF, BLOCK)
    both = factor_half(square[low, low])
    r00, v00 = upper_part(both[:, :HALF]), both[:, HALF:]
    r01 = dot(v00, square[low, high])
    both = factor_half(square[high, high] - dot(r01, r01, FIRST))
    r11, v11 = upper_part(both[:, :HALF]), both[:, HALF:]
    v10 = -dot(v11, dot(r01, v00, FIRST))
    zero = jnp.zeros((HALF, HALF), jnp.float32)
    factor = jnp.concatenate(
        [jnp.concatenate([r00, r01], axis=1), jnp.concatenate([zero, r11], axis=1)], axis=0
    )
    inverse = jnp.concatenate(
        [jnp.concatenate([v00, zero], axis=1), jnp.concatenate([v10, v11], axis=1)], axis=0
    )
    return factor, inverse


def pack_kernel(partners, waited, place_ref, field_ref, *refs):
    piece_refs = refs[waited:]
    slab = piece_refs[0].shape[1]
    for partner, piece_ref in zip(partners, piece_refs):
        start = lax.bitwise_xor(place_ref[0], partner) * slab
        piece_ref[...] = field_ref[:, pl.ds(pl.multiple_of(start, LANES), slab)]


def gram_kernel(place_ref, *refs):
    *piece_refs, base_ref, anomaly_ref, gram_ref = refs
    count = anomaly_ref.shape[0] // BLOCK
    base = base_ref[...].astype(jnp.float32)
    for partner, piece_ref in enumerate(piece_refs):
        size = piece_ref.shape[0]
        start = lax.bitwise_xor(place_ref[0], partner) * size if len(piece_refs) > 1 else 0
        anomaly_ref[pl.ds(pl.multiple_of(start, size), size), :] = (
            piece_ref[...].astype(jnp.float32) - base
        ).astype(jnp.bfloat16)
    at = 0
    for i in range(count):
        rows = anomaly_ref[pl.ds(i * BLOCK, BLOCK), :]
        rest = anomaly_ref[pl.ds(i * BLOCK, (count - i) * BLOCK), :]
        part = lax.dot_general(rows, rest, LAST, preferred_element_type=jnp.float32)
        for j in range(count - i):
            gram_ref[pl.ds(at * BLOCK, BLOCK), :] = part[:, j * BLOCK : (j + 1) * BLOCK]
            at += 1


def factor_kernel(
    scale, place_ref, mine_ref, other_ref, design_ref, anomaly_ref, basis_ref, factor_ref, gram_ref, inv_ref
):
    count = factor_ref.shape[0] // BLOCK
    slots, size = mine_ref.shape[0], mine_ref.shape[1]
    half, quarter = place_ref[0], place_ref[1]
    for slot in range(slots):
        piece = lax.bitwise_xor(quarter, slot)
        for side, ref in ((half, mine_ref), (1 - half, other_ref)):
            start = pl.multiple_of((side * slots + piece) * size, 8)
            gram_ref[pl.ds(start, size), :] = ref[slot] * scale
    pairs = upper_pairs(count)
    where = {pair: at for at, pair in enumerate(pairs)}

    def gram_at(i, j):
        return pl.ds(where[i, j] * BLOCK, BLOCK)

    def span(i):
        return pl.ds(i * BLOCK, BLOCK)

    for k in range(count):
        factor, inverse = factor_block(gram_ref[gram_at(k, k), :])
        factor_ref[span(k), span(k)] = factor
        rows = {}
        for j in range(k + 1, count):
            rows[j] = dot(inverse, gram_ref[gram_at(k, j), :])
            factor_ref[span(k), span(j)] = rows[j]
            factor_ref[span(j), span(k)] = jnp.zeros((BLOCK, BLOCK), jnp.float32)
        for i in range(k + 1, count):
            for j in range(i, count):
                gram_ref[gram_at(i, j), :] = gram_ref[gram_at(i, j), :] - dot(
                    rows[i], rows[j], FIRST
                )
        done = {}
        for j in range(k):
            done[j] = dot(inverse, inv_ref[span(k), span(j)])
            inv_ref[span(k), span(j)] = done[j]
        done[k] = inverse
        inv_ref[span(k), span(k)] = inverse
        for i in range(k + 1, count):
            for j in range(k + 1):
                old = inv_ref[span(i), span(j)] if j < k else 0.0
                inv_ref[span(i), span(j)] = old - dot(rows[i], done[j], FIRST)
    columns = []
    for j in range(count):
        tail = pl.ds(j * BLOCK, (count - j) * BLOCK)
        columns.append(dot(design_ref[tail, :], inv_ref[tail, span(j)], FIRST))
    mixing = jnp.concatenate(columns, axis=1).astype(jnp.bfloat16)
    basis_ref[...] = lax.dot_general(
        mixing, anomaly_ref[...], NARROW, preferred_element_type=jnp.float32
    ).astype(jnp.bfloat16)


def swap(value, mask, devices):
    return lax.ppermute(value, AXES, [(i, i ^ mask) for i in range(devices)])


def shards(snapshots, base_field, design):
    n_cells, n_rep = lax.axis_size("cells"), lax.axis_size("rep")
    devices = n_cells * n_rep
    local_runs = snapshots.shape[0]
    runs, modes = design.shape
    slab = base_field.shape[1]
    blocks = runs // BLOCK
    packed = len(upper_pairs(blocks)) * BLOCK
    vmem = pl.BlockSpec(memory_space=pltpu.VMEM)
    smem = pl.BlockSpec(memory_space=pltpu.SMEM)
    column = lax.axis_index("cells").astype(jnp.int32).reshape(1)
    if n_cells == 8 and local_runs % 16 == 0:
        field = snapshots.reshape(local_runs, n_cells * slab)
        pieces = {}
        for partners, after in (((4, 5, 3, 0), ()), ((6, 7, 2, 1), (3,))):
            packed_pieces = pl.pallas_call(
                functools.partial(pack_kernel, partners, len(after)),
                out_shape=[jax.ShapeDtypeStruct((local_runs, slab), jnp.bfloat16)] * len(partners),
                in_specs=[smem, vmem] + [pl.BlockSpec(memory_space=pl.ANY)] * len(after),
                out_specs=[vmem] * len(partners),
                compiler_params=pltpu.CompilerParams(vmem_limit_bytes=16 * 2**20),
            )(column, field, *[pieces[m] for m in after])
            for m, piece in zip(partners, packed_pieces):
                route = [(i, i ^ m) for i in range(n_cells)]
                pieces[m] = lax.ppermute(piece, "cells", route) if m else piece
        panel = [pieces[m] for m in range(n_cells)]
    else:
        slabs = snapshots.reshape(local_runs, n_cells, slab).transpose(1, 0, 2)
        moved = lax.all_to_all(slabs, "cells", split_axis=0, concat_axis=0, tiled=True)
        panel = [moved.reshape(runs, slab)]
    anomaly, gram = pl.pallas_call(
        gram_kernel,
        out_shape=(
            jax.ShapeDtypeStruct((runs, slab), jnp.bfloat16),
            jax.ShapeDtypeStruct((packed, LANES), jnp.float32),
        ),
        in_specs=[smem] + [vmem] * (len(panel) + 1),
        out_specs=(vmem, vmem),
        compiler_params=pltpu.CompilerParams(vmem_limit_bytes=32 * 2**20),
    )(column, *panel, base_field)

    me = lax.axis_index("cells") * n_rep + lax.axis_index("rep")
    half, quarter = me % 2, (me // 2) % 4
    halves = gram.reshape(2, packed // 2, LANES)
    got = swap(lax.dynamic_index_in_dim(halves, 1 - half, 0, keepdims=False), 1, devices)
    own = lax.dynamic_index_in_dim(halves, half, 0, keepdims=False) + got
    quarters = own.reshape(4, packed // 8, LANES)
    total = lax.dynamic_index_in_dim(quarters, quarter, 0, keepdims=False)
    parts = [
        swap(lax.dynamic_index_in_dim(quarters, quarter ^ m, 0, keepdims=False), 2 * m, devices)
        for m in (1, 2, 3)
    ]
    for part in parts:
        total = total + part
    mask = 8
    while mask < devices:
        total = total + swap(total, mask, devices)
        mask *= 2
    mine = jnp.stack([total] + [swap(total, 2 * m, devices) for m in (1, 2, 3)])
    other = swap(mine, 1, devices)

    def kernel(*refs):
        factor_kernel(1.0 / (slab * devices), *refs)

    basis, factor = pl.pallas_call(
        kernel,
        out_shape=(
            jax.ShapeDtypeStruct((modes, slab), jnp.bfloat16),
            jax.ShapeDtypeStruct((runs, runs), jnp.float32),
        ),
        in_specs=[smem, vmem, vmem, vmem, vmem],
        out_specs=(vmem, vmem),
        scratch_shapes=[
            pltpu.VMEM((packed, LANES), jnp.float32),
            pltpu.VMEM((runs, runs), jnp.float32),
        ],
        compiler_params=pltpu.CompilerParams(vmem_limit_bytes=32 * 2**20),
    )(jnp.stack([half, quarter]).astype(jnp.int32), mine, other, design, anomaly)
    return (basis.reshape(modes, 1, slab), factor)


def solution(mesh):
    in_specs = (P("cells", "rep", None), P("rep", "cells"), P())
    out_specs = (P(None, "rep", "cells"), P())
    return jax.shard_map(shards, mesh=mesh, in_specs=in_specs, out_specs=out_specs, check_vma=False)
```

```python
import functools

import jax
import jax.numpy as jnp
from jax import lax
from jax.experimental import pallas as pl
from jax.experimental.pallas import tpu as pltpu
from jax.sharding import PartitionSpec as P

BLOCK = 128
HALF = BLOCK // 2
LANES = 128
AXES = ("cells", "rep")
HIGH = lax.Precision.HIGHEST
NARROW = (((1,), (0,)), ((), ()))
FIRST = (((0,), (0,)), ((), ()))
LAST = (((1,), (1,)), ((), ()))


def dot(a, b, dims=NARROW):
    return lax.dot_general(a, b, dims, precision=HIGH, preferred_element_type=jnp.float32)


def upper_pairs(count):
    return [(i, j) for i in range(count) for j in range(i, count)]


def factor_half(rows, shift, work):
    tile = (8, LANES)
    sub = lax.broadcasted_iota(jnp.int32, tile, 0)
    both = jnp.where(own_lanes(shift), rows, unit_rows(HALF - shift))
    count = HALF // 8
    strips = [both[8 * j : 8 * j + 8, :] for j in range(count)]

    def spread_row(value, at):
        return jnp.broadcast_to(value[at : at + 1, :], tile)

    def spread_column(value, at):
        return jnp.broadcast_to(value[:, shift + at : shift + at + 1], tile)

    ahead = [spread_column(strips[0], t) for t in range(8)]
    for m in range(count):
        columns, near = ahead, {}
        close = range(m + 1, min(m + 1 + 8, count))
        for j in close:
            for t in range(8):
                near[j, t] = spread_column(strips[j], 8 * m + t)
        if m + 1 < count:
            ahead = [spread_column(strips[m + 1], 8 * m + 8 + t) for t in range(8)]
        corner = {(t, u): spread_row(columns[u], t) for t in range(8) for u in range(t, 8)}
        rows_left = [spread_row(strips[m], t) for t in range(8)]
        lines = []
        for t in range(8):
            root = lax.rsqrt(corner[t, t])
            line = {u: corner[t, u] * root for u in range(t + 1, 8)}
            for u in range(t + 1, 8):
                for v in range(u, 8):
                    corner[u, v] = corner[u, v] - line[u] * line[v]
            row = rows_left[t] * root
            lines.append(row)
            for u in range(t + 1, 8):
                rows_left[u] = rows_left[u] - line[u] * row
            for j in close:
                column = near[j, t] * root
                for u in range(t + 1, 8):
                    near[j, u] = near[j, u] - column * line[u]
                strips[j] = strips[j] - column * row
                if j == m + 1:
                    ahead = [ahead[u] - column * spread_row(column, u) for u in range(8)]
        done = lines[0]
        for t in range(1, 8):
            done = jnp.where(sub == t, lines[t], done)
        strips[m] = done
        for _ in range(-(-len(work) // (count - m))):
            work.pop(0)()
    return jnp.concatenate(strips, axis=0)


def lane_index():
    return lax.broadcasted_iota(jnp.int32, (HALF, LANES), 1)


def row_index():
    return lax.broadcasted_iota(jnp.int32, (HALF, LANES), 0)


def own_lanes(shift):
    return lane_index() < HALF if shift == 0 else lane_index() >= HALF


def unit_rows(shift):
    return (lane_index() == row_index() + shift).astype(jnp.float32)


def pack_kernel(partners, waited, place_ref, field_ref, *refs):
    piece_refs = refs[waited:]
    slab = piece_refs[0].shape[1]
    for partner, piece_ref in zip(partners, piece_refs):
        start = lax.bitwise_xor(place_ref[0], partner) * slab
        piece_ref[...] = field_ref[:, pl.ds(pl.multiple_of(start, LANES), slab)]


def gram_kernel(place_ref, *refs):
    *piece_refs, base_ref, anomaly_ref, gram_ref = refs
    count = anomaly_ref.shape[0] // BLOCK
    base = base_ref[...].astype(jnp.float32)
    for partner, piece_ref in enumerate(piece_refs):
        size = piece_ref.shape[0]
        start = lax.bitwise_xor(place_ref[0], partner) * size if len(piece_refs) > 1 else 0
        anomaly_ref[pl.ds(pl.multiple_of(start, size), size), :] = (
            piece_ref[...].astype(jnp.float32) - base
        ).astype(jnp.bfloat16)
    at = 0
    for i in range(count):
        rows = anomaly_ref[pl.ds(i * BLOCK, BLOCK), :]
        rest = anomaly_ref[pl.ds(i * BLOCK, (count - i) * BLOCK), :]
        part = lax.dot_general(rows, rest, LAST, preferred_element_type=jnp.float32)
        for j in range(count - i):
            gram_ref[pl.ds(at * BLOCK, BLOCK), :] = part[:, j * BLOCK : (j + 1) * BLOCK]
            at += 1


def factor_kernel(
    scale,
    place_ref,
    mine_ref,
    other_ref,
    design_ref,
    anomaly_ref,
    basis_ref,
    out_ref,
    gram_ref,
    inv_ref,
    factor_ref,
    mix_ref,
    sems,
):
    count = factor_ref.shape[0] // BLOCK
    slots, size = mine_ref.shape[0], mine_ref.shape[1]
    half, quarter = place_ref[0], place_ref[1]
    for slot in range(slots):
        piece = lax.bitwise_xor(quarter, slot)
        for side, ref in ((half, mine_ref), (1 - half, other_ref)):
            start = pl.multiple_of((side * slots + piece) * size, 8)
            gram_ref[pl.ds(start, size), :] = ref[slot] * scale
    where = {pair: at for at, pair in enumerate(upper_pairs(count))}
    zero = jnp.zeros((HALF, LANES), jnp.float32)

    def gram_at(i, j, side=None):
        start = where[i, j] * BLOCK
        return pl.ds(start, BLOCK) if side is None else pl.ds(start + side * HALF, HALF)

    def span(i, side=None):
        return pl.ds(i * BLOCK, BLOCK) if side is None else pl.ds(i * BLOCK + side * HALF, HALF)

    def apply(solved, side, rows):
        return dot(solved, jnp.concatenate([zero, rows] if side == 0 else [rows, zero], axis=0))

    def row_factor(k, side, solved, j):
        def run():
            factor_ref[span(k, side), span(j)] = apply(solved, side, gram_ref[gram_at(k, j, side), :])

        return run

    def row_inverse(k, side, solved, j):
        def run():
            if j < k:
                rows = inv_ref[span(k, side), span(j)]
            elif side == 0:
                rows = unit_rows(0)
            else:
                rows = inv_ref[span(k, 1), span(k)] + unit_rows(HALF)
            inv_ref[span(k, side), span(j)] = apply(solved, side, rows)

        return run

    def lower_gram(k, first, j):
        def run():
            part = dot(first, factor_ref[span(k, 0), span(j)], FIRST)[HALF:, :]
            gram_ref[gram_at(k, j, 1), :] = gram_ref[gram_at(k, j, 1), :] - part

        return run

    def lower_inverse(k, first, j):
        def run():
            part = dot(first, inv_ref[span(k, 0), span(j)], FIRST)[HALF:, :]
            old = inv_ref[span(k, 1), span(j)] if j < k else 0.0
            inv_ref[span(k, 1), span(j)] = old - part

        return run

    def next_gram(k, side):
        def run():
            rows = factor_ref[span(k, side), span(k + 1)]
            at = gram_at(k + 1, k + 1)
            gram_ref[at, :] = gram_ref[at, :] - dot(rows, rows, FIRST)

        return run

    def later_gram(k, i, j):
        def run():
            part = dot(factor_ref[span(k), span(i)], factor_ref[span(k), span(j)], FIRST)
            gram_ref[gram_at(i, j), :] = gram_ref[gram_at(i, j), :] - part

        return run

    def later_inverse(k, i, j):
        def run():
            part = dot(factor_ref[span(k), span(i)], inv_ref[span(k), span(j)], FIRST)
            old = inv_ref[span(i), span(j)] if j < k else 0.0
            inv_ref[span(i), span(j)] = old - part

        return run

    def mix(k, j):
        def run():
            part = dot(design_ref[span(k), :], inv_ref[span(k), span(j)], FIRST)
            mix_ref[:, span(j)] = part if j == k else mix_ref[:, span(j)] + part

        return run

    def send(k):
        return pltpu.make_async_copy(
            factor_ref.at[span(k), :], out_ref.at[span(k), :], sems.at[k]
        )

    work = []
    for k in range(count):
        for j in range(k):
            factor_ref[span(k), span(j)] = jnp.zeros((BLOCK, BLOCK), jnp.float32)
        solved = factor_half(gram_ref[gram_at(k, k, 0), :], 0, work)
        first = apply(solved, 0, gram_ref[gram_at(k, k, 0), :])
        lower = gram_ref[gram_at(k, k, 1), :] - dot(first, first, FIRST)[HALF:, :]
        first = jnp.where(
            own_lanes(0), jnp.where(lane_index() >= row_index(), solved, 0.0), first
        )
        factor_ref[span(k, 0), span(k)] = first
        for j in range(k + 1, count):
            work += [row_factor(k, 0, solved, j), lower_gram(k, first, j)]
            if j == k + 1:
                work.append(next_gram(k, 0))
        for j in range(k + 1):
            work += [row_inverse(k, 0, solved, j), lower_inverse(k, first, j)]
        solved = factor_half(lower, HALF, work)
        factor_ref[span(k, 1), span(k)] = jnp.where(
            lane_index() >= row_index() + HALF, solved, 0.0
        )
        if k + 1 < count:
            row_factor(k, 1, solved, k + 1)()
            next_gram(k, 1)()
        for j in range(k + 2, count):
            work.append(row_factor(k, 1, solved, j))
        work.append(send(k).start)
        for i in range(k + 1, count):
            work += [later_gram(k, i, j) for j in range(i, count) if (i, j) != (k + 1, k + 1)]
        work += [row_inverse(k, 1, solved, j) for j in range(k + 1)]
        for i in range(k + 1, count):
            work += [later_inverse(k, i, j) for j in range(k + 1)]
        work += [mix(k, j) for j in range(k + 1)]
    while work:
        work.pop(0)()
    basis_ref[...] = lax.dot_general(
        mix_ref[...].astype(jnp.bfloat16),
        anomaly_ref[...],
        NARROW,
        preferred_element_type=jnp.float32,
    ).astype(jnp.bfloat16)
    for k in range(count):
        send(k).wait()


def swap(value, mask, devices):
    return lax.ppermute(value, AXES, [(i, i ^ mask) for i in range(devices)])


def shards(snapshots, base_field, design):
    n_cells, n_rep = lax.axis_size("cells"), lax.axis_size("rep")
    devices = n_cells * n_rep
    local_runs = snapshots.shape[0]
    runs, modes = design.shape
    slab = base_field.shape[1]
    blocks = runs // BLOCK
    packed = len(upper_pairs(blocks)) * BLOCK
    vmem = pl.BlockSpec(memory_space=pltpu.VMEM)
    smem = pl.BlockSpec(memory_space=pltpu.SMEM)
    column = lax.axis_index("cells").astype(jnp.int32).reshape(1)
    if n_cells == 8 and local_runs % 16 == 0:
        field = snapshots.reshape(local_runs, n_cells * slab)
        pieces = {}
        for partners, after in (((4, 5, 3, 0), ()), ((6, 7, 2, 1), (3,))):
            packed_pieces = pl.pallas_call(
                functools.partial(pack_kernel, partners, len(after)),
                out_shape=[jax.ShapeDtypeStruct((local_runs, slab), jnp.bfloat16)] * len(partners),
                in_specs=[smem, vmem] + [pl.BlockSpec(memory_space=pl.ANY)] * len(after),
                out_specs=[vmem] * len(partners),
                compiler_params=pltpu.CompilerParams(vmem_limit_bytes=16 * 2**20),
            )(column, field, *[pieces[m] for m in after])
            for m, piece in zip(partners, packed_pieces):
                route = [(i, i ^ m) for i in range(n_cells)]
                pieces[m] = lax.ppermute(piece, "cells", route) if m else piece
        panel = [pieces[m] for m in range(n_cells)]
    else:
        slabs = snapshots.reshape(local_runs, n_cells, slab).transpose(1, 0, 2)
        moved = lax.all_to_all(slabs, "cells", split_axis=0, concat_axis=0, tiled=True)
        panel = [moved.reshape(runs, slab)]
    anomaly, gram = pl.pallas_call(
        gram_kernel,
        out_shape=(
            jax.ShapeDtypeStruct((runs, slab), jnp.bfloat16),
            jax.ShapeDtypeStruct((packed, LANES), jnp.float32),
        ),
        in_specs=[smem] + [vmem] * (len(panel) + 1),
        out_specs=(vmem, vmem),
        compiler_params=pltpu.CompilerParams(vmem_limit_bytes=32 * 2**20),
    )(column, *panel, base_field)

    me = lax.axis_index("cells") * n_rep + lax.axis_index("rep")
    half, quarter = me % 2, (me // 2) % 4
    halves = gram.reshape(2, packed // 2, LANES)
    got = swap(lax.dynamic_index_in_dim(halves, 1 - half, 0, keepdims=False), 1, devices)
    own = lax.dynamic_index_in_dim(halves, half, 0, keepdims=False) + got
    quarters = own.reshape(4, packed // 8, LANES)
    total = lax.dynamic_index_in_dim(quarters, quarter, 0, keepdims=False)
    parts = [
        swap(lax.dynamic_index_in_dim(quarters, quarter ^ m, 0, keepdims=False), 2 * m, devices)
        for m in (1, 2, 3)
    ]
    for part in parts:
        total = total + part
    mask = 8
    while mask < devices:
        total = total + swap(total, mask, devices)
        mask *= 2
    mine = jnp.stack([total] + [swap(total, 2 * m, devices) for m in (1, 2, 3)])
    other = swap(mine, 1, devices)

    def kernel(*refs):
        factor_kernel(1.0 / (slab * devices), *refs)

    basis, factor = pl.pallas_call(
        kernel,
        out_shape=(
            jax.ShapeDtypeStruct((modes, slab), jnp.bfloat16),
            jax.ShapeDtypeStruct((runs, runs), jnp.float32),
        ),
        in_specs=[smem, vmem, vmem, vmem, vmem],
        out_specs=(vmem, pl.BlockSpec(memory_space=pl.ANY)),
        scratch_shapes=[
            pltpu.VMEM((packed, LANES), jnp.float32),
            pltpu.VMEM((runs, runs), jnp.float32),
            pltpu.VMEM((runs, runs), jnp.float32),
            pltpu.VMEM((modes, runs), jnp.float32),
            pltpu.SemaphoreType.DMA((blocks,)),
        ],
        compiler_params=pltpu.CompilerParams(vmem_limit_bytes=32 * 2**20),
    )(jnp.stack([half, quarter]).astype(jnp.int32), mine, other, design, anomaly)
    return (basis.reshape(modes, 1, slab), factor)


def solution(mesh):
    in_specs = (P("cells", "rep", None), P("rep", "cells"), P())
    out_specs = (P(None, "rep", "cells"), P())
    return jax.shard_map(shards, mesh=mesh, in_specs=in_specs, out_specs=out_specs, check_vma=False)
```

```python
import functools

import jax
import jax.numpy as jnp
from jax import lax
from jax.experimental import pallas as pl
from jax.experimental.pallas import tpu as pltpu
from jax.sharding import PartitionSpec as P

BLOCK = 128
HALF = BLOCK // 2
LANES = 128
AXES = ("cells", "rep")
HIGH = lax.Precision.HIGHEST
NARROW = (((1,), (0,)), ((), ()))
FIRST = (((0,), (0,)), ((), ()))
LAST = (((1,), (1,)), ((), ()))


def dot(a, b, dims=NARROW):
    return lax.dot_general(a, b, dims, precision=HIGH, preferred_element_type=jnp.float32)


def upper_pairs(count):
    return [(i, j) for i in range(count) for j in range(i, count)]


def packing(count):
    places, tails, at = {}, [], 0
    for i, j in upper_pairs(count):
        places[i, j] = at
        at += HALF if i == j else BLOCK
    for _ in range(count // 2):
        tails.append(at)
        at += HALF
    return places, tails, at


def factor_half(rows, shift, work):
    tile = (8, LANES)
    sub = lax.broadcasted_iota(jnp.int32, tile, 0)
    both = jnp.where(own_lanes(shift), rows, unit_rows(HALF - shift))
    count = HALF // 8
    strips = [both[8 * j : 8 * j + 8, :] for j in range(count)]

    def spread_row(value, at):
        return jnp.broadcast_to(value[at : at + 1, :], tile)

    def spread_column(value, at):
        return jnp.broadcast_to(value[:, shift + at : shift + at + 1], tile)

    ahead = [spread_column(strips[0], t) for t in range(8)]
    for m in range(count):
        columns, near = ahead, {}
        close = range(m + 1, min(m + 1 + 8, count))
        for j in close:
            for t in range(8):
                near[j, t] = spread_column(strips[j], 8 * m + t)
        if m + 1 < count:
            ahead = [spread_column(strips[m + 1], 8 * m + 8 + t) for t in range(8)]
        corner = {(t, u): spread_row(columns[u], t) for t in range(8) for u in range(t, 8)}
        rows_left = [spread_row(strips[m], t) for t in range(8)]
        lines = []
        for t in range(8):
            root = lax.rsqrt(corner[t, t])
            line = {u: corner[t, u] * root for u in range(t + 1, 8)}
            for u in range(t + 1, 8):
                for v in range(u, 8):
                    corner[u, v] = corner[u, v] - line[u] * line[v]
            row = rows_left[t] * root
            lines.append(row)
            for u in range(t + 1, 8):
                rows_left[u] = rows_left[u] - line[u] * row
            for j in close:
                column = near[j, t] * root
                for u in range(t + 1, 8):
                    near[j, u] = near[j, u] - column * line[u]
                strips[j] = strips[j] - column * row
                if j == m + 1:
                    ahead = [ahead[u] - column * spread_row(column, u) for u in range(8)]
        done = lines[0]
        for t in range(1, 8):
            done = jnp.where(sub == t, lines[t], done)
        strips[m] = done
        for _ in range(-(-len(work) // (count - m))):
            work.pop(0)()
    return jnp.concatenate(strips, axis=0)


def lane_index():
    return lax.broadcasted_iota(jnp.int32, (HALF, LANES), 1)


def row_index():
    return lax.broadcasted_iota(jnp.int32, (HALF, LANES), 0)


def own_lanes(shift):
    return lane_index() < HALF if shift == 0 else lane_index() >= HALF


def unit_rows(shift):
    return (lane_index() == row_index() + shift).astype(jnp.float32)


def pack_kernel(partners, waited, place_ref, field_ref, *refs):
    piece_refs = refs[waited:]
    slab = piece_refs[0].shape[1]
    for partner, piece_ref in zip(partners, piece_refs):
        start = lax.bitwise_xor(place_ref[0], partner) * slab
        piece_ref[...] = field_ref[:, pl.ds(pl.multiple_of(start, LANES), slab)]


def gram_kernel(place_ref, *refs):
    *piece_refs, base_ref, anomaly_ref, gram_ref = refs
    count = anomaly_ref.shape[0] // BLOCK
    base = base_ref[...].astype(jnp.float32)
    for partner, piece_ref in enumerate(piece_refs):
        size = piece_ref.shape[0]
        start = lax.bitwise_xor(place_ref[0], partner) * size if len(piece_refs) > 1 else 0
        anomaly_ref[pl.ds(pl.multiple_of(start, size), size), :] = (
            piece_ref[...].astype(jnp.float32) - base
        ).astype(jnp.bfloat16)
    places, tails, _ = packing(count)
    kept = None
    for i in range(count):
        rows = anomaly_ref[pl.ds(i * BLOCK, BLOCK), :]
        rest = anomaly_ref[pl.ds(i * BLOCK, (count - i) * BLOCK), :]
        part = lax.dot_general(rows, rest, LAST, preferred_element_type=jnp.float32)
        gram_ref[pl.ds(places[i, i], HALF), :] = part[:HALF, :BLOCK]
        for j in range(i + 1, count):
            at = (j - i) * BLOCK
            gram_ref[pl.ds(places[i, j], BLOCK), :] = part[:, at : at + BLOCK]
        corner = part[HALF:, HALF:BLOCK]
        if i % 2 == 0:
            kept = corner
        else:
            gram_ref[pl.ds(tails[i // 2], HALF), :] = jnp.concatenate([kept, corner], axis=1)


def factor_kernel(
    scale,
    place_ref,
    piece_refs,
    design_ref,
    anomaly_ref,
    basis_ref,
    out_ref,
    packed_ref,
    gram_ref,
    inv_ref,
    factor_ref,
    mix_ref,
    sems,
):
    count = factor_ref.shape[0] // BLOCK
    slots, size = len(piece_refs) // 2, piece_refs[0].shape[0]
    half, quarter = place_ref[0], place_ref[1]
    for slot in range(slots):
        piece = lax.bitwise_xor(quarter, slot)
        for side, ref in ((half, piece_refs[slot]), (1 - half, piece_refs[slots + slot])):
            start = pl.multiple_of((side * slots + piece) * size, 8)
            packed_ref[pl.ds(start, size), :] = ref[...] * scale
    places, tails, _ = packing(count)
    where = {pair: at for at, pair in enumerate(upper_pairs(count))}
    for (i, j), at in where.items():
        size = HALF if i == j else BLOCK
        gram_ref[pl.ds(at * BLOCK, size), :] = packed_ref[pl.ds(places[i, j], size), :]
        if i == j:
            corner = packed_ref[pl.ds(tails[i // 2], HALF), :]
            if i % 2 == 0:
                corner = jnp.concatenate([corner[:, :HALF], corner[:, :HALF]], axis=1)
            gram_ref[pl.ds(at * BLOCK + HALF, HALF), :] = corner
    zero = jnp.zeros((HALF, LANES), jnp.float32)

    def gram_at(i, j, side=None):
        start = where[i, j] * BLOCK
        return pl.ds(start, BLOCK) if side is None else pl.ds(start + side * HALF, HALF)

    def span(i, side=None):
        return pl.ds(i * BLOCK, BLOCK) if side is None else pl.ds(i * BLOCK + side * HALF, HALF)

    def apply(solved, side, rows):
        return dot(solved, jnp.concatenate([zero, rows] if side == 0 else [rows, zero], axis=0))

    def row_factor(k, side, solved, j):
        def run():
            factor_ref[span(k, side), span(j)] = apply(solved, side, gram_ref[gram_at(k, j, side), :])

        return run

    def row_inverse(k, side, solved, j):
        def run():
            if j < k:
                rows = inv_ref[span(k, side), span(j)]
            elif side == 0:
                rows = unit_rows(0)
            else:
                rows = inv_ref[span(k, 1), span(k)] + unit_rows(HALF)
            inv_ref[span(k, side), span(j)] = apply(solved, side, rows)

        return run

    def lower_gram(k, first, j):
        def run():
            part = dot(first, factor_ref[span(k, 0), span(j)], FIRST)[HALF:, :]
            gram_ref[gram_at(k, j, 1), :] = gram_ref[gram_at(k, j, 1), :] - part

        return run

    def lower_inverse(k, first, j):
        def run():
            part = dot(first, inv_ref[span(k, 0), span(j)], FIRST)[HALF:, :]
            old = inv_ref[span(k, 1), span(j)] if j < k else 0.0
            inv_ref[span(k, 1), span(j)] = old - part

        return run

    def next_gram(k, side):
        def run():
            rows = factor_ref[span(k, side), span(k + 1)]
            at = gram_at(k + 1, k + 1)
            gram_ref[at, :] = gram_ref[at, :] - dot(rows, rows, FIRST)

        return run

    def later_gram(k, i, j):
        def run():
            part = dot(factor_ref[span(k), span(i)], factor_ref[span(k), span(j)], FIRST)
            gram_ref[gram_at(i, j), :] = gram_ref[gram_at(i, j), :] - part

        return run

    def later_inverse(k, i, j):
        def run():
            part = dot(factor_ref[span(k), span(i)], inv_ref[span(k), span(j)], FIRST)
            old = inv_ref[span(i), span(j)] if j < k else 0.0
            inv_ref[span(i), span(j)] = old - part

        return run

    def mix(k, j):
        def run():
            part = dot(design_ref[span(k), :], inv_ref[span(k), span(j)], FIRST)
            mix_ref[:, span(j)] = part if j == k else mix_ref[:, span(j)] + part

        return run

    def send(k):
        return pltpu.make_async_copy(
            factor_ref.at[span(k), :], out_ref.at[span(k), :], sems.at[k]
        )

    work = []
    for k in range(count):
        for j in range(k):
            factor_ref[span(k), span(j)] = jnp.zeros((BLOCK, BLOCK), jnp.float32)
        solved = factor_half(gram_ref[gram_at(k, k, 0), :], 0, work)
        first = apply(solved, 0, gram_ref[gram_at(k, k, 0), :])
        lower = gram_ref[gram_at(k, k, 1), :] - dot(first, first, FIRST)[HALF:, :]
        first = jnp.where(
            own_lanes(0), jnp.where(lane_index() >= row_index(), solved, 0.0), first
        )
        factor_ref[span(k, 0), span(k)] = first
        for j in range(k + 1, count):
            work += [row_factor(k, 0, solved, j), lower_gram(k, first, j)]
            if j == k + 1:
                work.append(next_gram(k, 0))
        for j in range(k + 1):
            work += [row_inverse(k, 0, solved, j), lower_inverse(k, first, j)]
        solved = factor_half(lower, HALF, work)
        factor_ref[span(k, 1), span(k)] = jnp.where(
            lane_index() >= row_index() + HALF, solved, 0.0
        )
        if k + 1 < count:
            row_factor(k, 1, solved, k + 1)()
            next_gram(k, 1)()
        for j in range(k + 2, count):
            work.append(row_factor(k, 1, solved, j))
        work.append(send(k).start)
        for i in range(k + 1, count):
            work += [later_gram(k, i, j) for j in range(i, count) if (i, j) != (k + 1, k + 1)]
        work += [row_inverse(k, 1, solved, j) for j in range(k + 1)]
        for i in range(k + 1, count):
            work += [later_inverse(k, i, j) for j in range(k + 1)]
        work += [mix(k, j) for j in range(k + 1)]
    while work:
        work.pop(0)()
    basis_ref[...] = lax.dot_general(
        mix_ref[...].astype(jnp.bfloat16),
        anomaly_ref[...],
        NARROW,
        preferred_element_type=jnp.float32,
    ).astype(jnp.bfloat16)
    for k in range(count):
        send(k).wait()


def swap(value, mask, devices):
    return lax.ppermute(value, AXES, [(i, i ^ mask) for i in range(devices)])


def shards(snapshots, base_field, design):
    n_cells, n_rep = lax.axis_size("cells"), lax.axis_size("rep")
    devices = n_cells * n_rep
    local_runs = snapshots.shape[0]
    runs, modes = design.shape
    slab = base_field.shape[1]
    blocks = runs // BLOCK
    packed = packing(blocks)[2]
    vmem = pl.BlockSpec(memory_space=pltpu.VMEM)
    smem = pl.BlockSpec(memory_space=pltpu.SMEM)
    column = lax.axis_index("cells").astype(jnp.int32).reshape(1)
    if n_cells == 8 and local_runs % 16 == 0:
        field = snapshots.reshape(local_runs, n_cells * slab)
        pieces = {}
        for partners, after in (((4, 5, 3, 0), ()), ((6, 7, 2, 1), (3,))):
            packed_pieces = pl.pallas_call(
                functools.partial(pack_kernel, partners, len(after)),
                out_shape=[jax.ShapeDtypeStruct((local_runs, slab), jnp.bfloat16)] * len(partners),
                in_specs=[smem, vmem] + [pl.BlockSpec(memory_space=pl.ANY)] * len(after),
                out_specs=[vmem] * len(partners),
                compiler_params=pltpu.CompilerParams(vmem_limit_bytes=16 * 2**20),
            )(column, field, *[pieces[m] for m in after])
            for m, piece in zip(partners, packed_pieces):
                route = [(i, i ^ m) for i in range(n_cells)]
                pieces[m] = lax.ppermute(piece, "cells", route) if m else piece
        panel = [pieces[m] for m in range(n_cells)]
    else:
        slabs = snapshots.reshape(local_runs, n_cells, slab).transpose(1, 0, 2)
        moved = lax.all_to_all(slabs, "cells", split_axis=0, concat_axis=0, tiled=True)
        panel = [moved.reshape(runs, slab)]
    anomaly, gram = pl.pallas_call(
        gram_kernel,
        out_shape=(
            jax.ShapeDtypeStruct((runs, slab), jnp.bfloat16),
            jax.ShapeDtypeStruct((packed, LANES), jnp.float32),
        ),
        in_specs=[smem] + [vmem] * (len(panel) + 1),
        out_specs=(vmem, vmem),
        compiler_params=pltpu.CompilerParams(vmem_limit_bytes=32 * 2**20),
    )(column, *panel, base_field)

    me = lax.axis_index("cells") * n_rep + lax.axis_index("rep")
    half, quarter = me % 2, (me // 2) % 4
    halves = gram.reshape(2, packed // 2, LANES)
    got = swap(lax.dynamic_index_in_dim(halves, 1 - half, 0, keepdims=False), 1, devices)
    own = lax.dynamic_index_in_dim(halves, half, 0, keepdims=False) + got
    quarters = own.reshape(4, packed // 8, LANES)
    total = lax.dynamic_index_in_dim(quarters, quarter, 0, keepdims=False)
    parts = [
        swap(lax.dynamic_index_in_dim(quarters, quarter ^ m, 0, keepdims=False), 2 * m, devices)
        for m in (1, 2, 3)
    ]
    for part in parts:
        total = total + part
    mask = 8
    while mask < devices:
        total = total + swap(total, mask, devices)
        mask *= 2
    mine = [total] + [swap(total, 2 * m, devices) for m in (1, 2, 3)]
    other = [swap(piece, 1, devices) for piece in mine]

    def kernel(*refs):
        factor_kernel(1.0 / (slab * devices), refs[0], refs[1:9], *refs[9:])

    basis, factor = pl.pallas_call(
        kernel,
        out_shape=(
            jax.ShapeDtypeStruct((modes, slab), jnp.bfloat16),
            jax.ShapeDtypeStruct((runs, runs), jnp.float32),
        ),
        in_specs=[smem] + [vmem] * 10,
        out_specs=(vmem, pl.BlockSpec(memory_space=pl.ANY)),
        scratch_shapes=[
            pltpu.VMEM((packed, LANES), jnp.float32),
            pltpu.VMEM((len(upper_pairs(blocks)) * BLOCK, LANES), jnp.float32),
            pltpu.VMEM((runs, runs), jnp.float32),
            pltpu.VMEM((runs, runs), jnp.float32),
            pltpu.VMEM((modes, runs), jnp.float32),
            pltpu.SemaphoreType.DMA((blocks,)),
        ],
        compiler_params=pltpu.CompilerParams(vmem_limit_bytes=32 * 2**20),
    )(jnp.stack([half, quarter]).astype(jnp.int32), *mine, *other, design, anomaly)
    return (basis.reshape(modes, 1, slab), factor)


def solution(mesh):
    in_specs = (P("cells", "rep", None), P("rep", "cells"), P())
    out_specs = (P(None, "rep", "cells"), P())
    return jax.shard_map(shards, mesh=mesh, in_specs=in_specs, out_specs=out_specs, check_vma=False)
```

```python
import functools

import jax
import jax.numpy as jnp
from jax import lax
from jax.experimental import pallas as pl
from jax.experimental.pallas import tpu as pltpu
from jax.sharding import PartitionSpec as P

BLOCK = 128
HALF = BLOCK // 2
LANES = 128
AXES = ("cells", "rep")
HIGH = lax.Precision.HIGHEST
NARROW = (((1,), (0,)), ((), ()))
FIRST = (((0,), (0,)), ((), ()))
LAST = (((1,), (1,)), ((), ()))


def dot(a, b, dims=NARROW):
    return lax.dot_general(a, b, dims, precision=HIGH, preferred_element_type=jnp.float32)


def upper_pairs(count):
    return [(i, j) for i in range(count) for j in range(i, count)]


def packing(count):
    places, tails, at = {}, [], 0
    for i, j in upper_pairs(count):
        places[i, j] = at
        at += HALF if i == j else BLOCK
    for _ in range(count // 2):
        tails.append(at)
        at += HALF
    return places, tails, at


def factor_half(rows, shift, work):
    tile = (8, LANES)
    sub = lax.broadcasted_iota(jnp.int32, tile, 0)
    both = jnp.where(own_lanes(shift), rows, unit_rows(HALF - shift))
    count = HALF // 8
    strips = [both[8 * j : 8 * j + 8, :] for j in range(count)]

    def spread_row(value, at):
        return jnp.broadcast_to(value[at : at + 1, :], tile)

    def spread_column(value, at):
        return jnp.broadcast_to(value[:, shift + at : shift + at + 1], tile)

    ahead = [spread_column(strips[0], t) for t in range(8)]
    for m in range(count):
        columns, near = ahead, {}
        close = range(m + 1, min(m + 1 + 8, count))
        for j in close:
            for t in range(8):
                near[j, t] = spread_column(strips[j], 8 * m + t)
        if m + 1 < count:
            ahead = [spread_column(strips[m + 1], 8 * m + 8 + t) for t in range(8)]
        corner = {(t, u): spread_row(columns[u], t) for t in range(8) for u in range(t, 8)}
        rows_left = [spread_row(strips[m], t) for t in range(8)]
        lines = []
        for t in range(8):
            root = lax.rsqrt(corner[t, t])
            line = {u: corner[t, u] * root for u in range(t + 1, 8)}
            for u in range(t + 1, 8):
                for v in range(u, 8):
                    corner[u, v] = corner[u, v] - line[u] * line[v]
            row = rows_left[t] * root
            lines.append(row)
            for u in range(t + 1, 8):
                rows_left[u] = rows_left[u] - line[u] * row
            for j in close:
                column = near[j, t] * root
                for u in range(t + 1, 8):
                    near[j, u] = near[j, u] - column * line[u]
                strips[j] = strips[j] - column * row
                if j == m + 1:
                    ahead = [ahead[u] - column * spread_row(column, u) for u in range(8)]
        done = lines[0]
        for t in range(1, 8):
            done = jnp.where(sub == t, lines[t], done)
        strips[m] = done
        for _ in range(-(-len(work) // (count - m))):
            work.pop(0)()
    return jnp.concatenate(strips, axis=0)


def lane_index():
    return lax.broadcasted_iota(jnp.int32, (HALF, LANES), 1)


def row_index():
    return lax.broadcasted_iota(jnp.int32, (HALF, LANES), 0)


def own_lanes(shift):
    return lane_index() < HALF if shift == 0 else lane_index() >= HALF


def unit_rows(shift):
    return (lane_index() == row_index() + shift).astype(jnp.float32)


def pack_kernel(partners, waited, place_ref, field_ref, *refs):
    piece_refs = refs[waited:]
    slab = piece_refs[0].shape[1]
    for partner, piece_ref in zip(partners, piece_refs):
        start = lax.bitwise_xor(place_ref[0], partner) * slab
        piece_ref[...] = field_ref[:, pl.ds(pl.multiple_of(start, LANES), slab)]


def gram_kernel(place_ref, *refs):
    *piece_refs, base_ref, anomaly_ref, gram_ref = refs
    count = anomaly_ref.shape[0] // BLOCK
    base = base_ref[...].astype(jnp.float32)
    for partner, piece_ref in enumerate(piece_refs):
        size = piece_ref.shape[0]
        start = lax.bitwise_xor(place_ref[0], partner) * size if len(piece_refs) > 1 else 0
        anomaly_ref[pl.ds(pl.multiple_of(start, size), size), :] = (
            piece_ref[...].astype(jnp.float32) - base
        ).astype(jnp.bfloat16)
    places, tails, _ = packing(count)
    kept = None
    for i in range(count):
        if i % 2 == 0:
            rows = anomaly_ref[pl.ds(i * BLOCK, 2 * BLOCK), :]
            rest = anomaly_ref[pl.ds(i * BLOCK, (count - i) * BLOCK), :]
            wide = lax.dot_general(rows, rest, LAST, preferred_element_type=jnp.float32)
        part = wide[:BLOCK, :] if i % 2 == 0 else wide[BLOCK:, BLOCK:]
        gram_ref[pl.ds(places[i, i], HALF), :] = part[:HALF, :BLOCK]
        for j in range(i + 1, count):
            at = (j - i) * BLOCK
            gram_ref[pl.ds(places[i, j], BLOCK), :] = part[:, at : at + BLOCK]
        corner = part[HALF:, HALF:BLOCK]
        if i % 2 == 0:
            kept = corner
        else:
            gram_ref[pl.ds(tails[i // 2], HALF), :] = jnp.concatenate([kept, corner], axis=1)


def factor_kernel(
    scale,
    place_ref,
    piece_refs,
    design_ref,
    anomaly_ref,
    basis_ref,
    out_ref,
    packed_ref,
    gram_ref,
    inv_ref,
    factor_ref,
    mix_ref,
    sems,
):
    count = factor_ref.shape[0] // BLOCK
    slots, size = len(piece_refs) // 2, piece_refs[0].shape[0]
    half, quarter = place_ref[0], place_ref[1]
    for slot in range(slots):
        piece = lax.bitwise_xor(quarter, slot)
        for side, ref in ((half, piece_refs[slot]), (1 - half, piece_refs[slots + slot])):
            start = pl.multiple_of((side * slots + piece) * size, 8)
            packed_ref[pl.ds(start, size), :] = ref[...] * scale
    places, tails, _ = packing(count)
    where = {pair: at for at, pair in enumerate(upper_pairs(count))}
    for (i, j), at in where.items():
        size = HALF if i == j else BLOCK
        gram_ref[pl.ds(at * BLOCK, size), :] = packed_ref[pl.ds(places[i, j], size), :]
        if i == j:
            corner = packed_ref[pl.ds(tails[i // 2], HALF), :]
            if i % 2 == 0:
                corner = jnp.concatenate([corner[:, :HALF], corner[:, :HALF]], axis=1)
            gram_ref[pl.ds(at * BLOCK + HALF, HALF), :] = corner
    zero = jnp.zeros((HALF, LANES), jnp.float32)

    def gram_at(i, j, side=None):
        start = where[i, j] * BLOCK
        return pl.ds(start, BLOCK) if side is None else pl.ds(start + side * HALF, HALF)

    def span(i, side=None):
        return pl.ds(i * BLOCK, BLOCK) if side is None else pl.ds(i * BLOCK + side * HALF, HALF)

    def apply(solved, side, rows):
        return dot(solved, jnp.concatenate([zero, rows] if side == 0 else [rows, zero], axis=0))

    def row_factor(k, side, solved, j):
        def run():
            factor_ref[span(k, side), span(j)] = apply(solved, side, gram_ref[gram_at(k, j, side), :])

        return run

    def row_inverse(k, side, solved, j):
        def run():
            if j < k:
                rows = inv_ref[span(k, side), span(j)]
            elif side == 0:
                rows = unit_rows(0)
            else:
                rows = inv_ref[span(k, 1), span(k)] + unit_rows(HALF)
            inv_ref[span(k, side), span(j)] = apply(solved, side, rows)

        return run

    def lower_gram(k, first, j):
        def run():
            part = dot(first, factor_ref[span(k, 0), span(j)], FIRST)[HALF:, :]
            gram_ref[gram_at(k, j, 1), :] = gram_ref[gram_at(k, j, 1), :] - part

        return run

    def lower_inverse(k, first, j):
        def run():
            part = dot(first, inv_ref[span(k, 0), span(j)], FIRST)[HALF:, :]
            old = inv_ref[span(k, 1), span(j)] if j < k else 0.0
            inv_ref[span(k, 1), span(j)] = old - part

        return run

    def next_gram(k, side):
        def run():
            rows = factor_ref[span(k, side), span(k + 1)]
            at = gram_at(k + 1, k + 1)
            gram_ref[at, :] = gram_ref[at, :] - dot(rows, rows, FIRST)

        return run

    def later_gram(k, i, j):
        def run():
            part = dot(factor_ref[span(k), span(i)], factor_ref[span(k), span(j)], FIRST)
            gram_ref[gram_at(i, j), :] = gram_ref[gram_at(i, j), :] - part

        return run

    def later_inverse(k, i, j):
        def run():
            part = dot(factor_ref[span(k), span(i)], inv_ref[span(k), span(j)], FIRST)
            old = inv_ref[span(i), span(j)] if j < k else 0.0
            inv_ref[span(i), span(j)] = old - part

        return run

    def mix(k, j):
        def run():
            part = dot(design_ref[span(k), :], inv_ref[span(k), span(j)], FIRST)
            mix_ref[:, span(j)] = part if j == k else mix_ref[:, span(j)] + part

        return run

    def send(k):
        return pltpu.make_async_copy(
            factor_ref.at[span(k), :], out_ref.at[span(k), :], sems.at[k]
        )

    work = []
    for k in range(count):
        for j in range(k):
            factor_ref[span(k), span(j)] = jnp.zeros((BLOCK, BLOCK), jnp.float32)
        solved = factor_half(gram_ref[gram_at(k, k, 0), :], 0, work)
        first = apply(solved, 0, gram_ref[gram_at(k, k, 0), :])
        lower = gram_ref[gram_at(k, k, 1), :] - dot(first, first, FIRST)[HALF:, :]
        first = jnp.where(
            own_lanes(0), jnp.where(lane_index() >= row_index(), solved, 0.0), first
        )
        factor_ref[span(k, 0), span(k)] = first
        for j in range(k + 1, count):
            work += [row_factor(k, 0, solved, j), lower_gram(k, first, j)]
            if j == k + 1:
                work.append(next_gram(k, 0))
        for j in range(k + 1):
            work += [row_inverse(k, 0, solved, j), lower_inverse(k, first, j)]
        solved = factor_half(lower, HALF, work)
        factor_ref[span(k, 1), span(k)] = jnp.where(
            lane_index() >= row_index() + HALF, solved, 0.0
        )
        if k + 1 < count:
            row_factor(k, 1, solved, k + 1)()
            next_gram(k, 1)()
        for j in range(k + 2, count):
            work.append(row_factor(k, 1, solved, j))
        work.append(send(k).start)
        for i in range(k + 1, count):
            work += [later_gram(k, i, j) for j in range(i, count) if (i, j) != (k + 1, k + 1)]
        work += [row_inverse(k, 1, solved, j) for j in range(k + 1)]
        for i in range(k + 1, count):
            work += [later_inverse(k, i, j) for j in range(k + 1)]
        work += [mix(k, j) for j in range(k + 1)]
    while work:
        work.pop(0)()
    basis_ref[...] = lax.dot_general(
        mix_ref[...].astype(jnp.bfloat16),
        anomaly_ref[...],
        NARROW,
        preferred_element_type=jnp.float32,
    ).astype(jnp.bfloat16)
    for k in range(count):
        send(k).wait()


def swap(value, mask, devices):
    return lax.ppermute(value, AXES, [(i, i ^ mask) for i in range(devices)])


def shards(snapshots, base_field, design):
    n_cells, n_rep = lax.axis_size("cells"), lax.axis_size("rep")
    devices = n_cells * n_rep
    local_runs = snapshots.shape[0]
    runs, modes = design.shape
    slab = base_field.shape[1]
    blocks = runs // BLOCK
    packed = packing(blocks)[2]
    vmem = pl.BlockSpec(memory_space=pltpu.VMEM)
    smem = pl.BlockSpec(memory_space=pltpu.SMEM)
    column = lax.axis_index("cells").astype(jnp.int32).reshape(1)
    if n_cells == 8 and local_runs % 16 == 0:
        field = snapshots.reshape(local_runs, n_cells * slab)
        pieces = {}
        for partners, after in (((4, 5, 3, 0), ()), ((6, 7, 2, 1), (3,))):
            packed_pieces = pl.pallas_call(
                functools.partial(pack_kernel, partners, len(after)),
                out_shape=[jax.ShapeDtypeStruct((local_runs, slab), jnp.bfloat16)] * len(partners),
                in_specs=[smem, vmem] + [pl.BlockSpec(memory_space=pl.ANY)] * len(after),
                out_specs=[vmem] * len(partners),
                compiler_params=pltpu.CompilerParams(vmem_limit_bytes=16 * 2**20),
            )(column, field, *[pieces[m] for m in after])
            for m, piece in zip(partners, packed_pieces):
                route = [(i, i ^ m) for i in range(n_cells)]
                pieces[m] = lax.ppermute(piece, "cells", route) if m else piece
        panel = [pieces[m] for m in range(n_cells)]
    else:
        slabs = snapshots.reshape(local_runs, n_cells, slab).transpose(1, 0, 2)
        moved = lax.all_to_all(slabs, "cells", split_axis=0, concat_axis=0, tiled=True)
        panel = [moved.reshape(runs, slab)]
    anomaly, gram = pl.pallas_call(
        gram_kernel,
        out_shape=(
            jax.ShapeDtypeStruct((runs, slab), jnp.bfloat16),
            jax.ShapeDtypeStruct((packed, LANES), jnp.float32),
        ),
        in_specs=[smem] + [vmem] * (len(panel) + 1),
        out_specs=(vmem, vmem),
        compiler_params=pltpu.CompilerParams(vmem_limit_bytes=32 * 2**20),
    )(column, *panel, base_field)

    me = lax.axis_index("cells") * n_rep + lax.axis_index("rep")
    half, quarter = me % 2, (me // 2) % 4
    halves = gram.reshape(2, packed // 2, LANES)
    got = swap(lax.dynamic_index_in_dim(halves, 1 - half, 0, keepdims=False), 1, devices)
    own = lax.dynamic_index_in_dim(halves, half, 0, keepdims=False) + got
    quarters = own.reshape(4, packed // 8, LANES)
    total = lax.dynamic_index_in_dim(quarters, quarter, 0, keepdims=False)
    parts = [
        swap(lax.dynamic_index_in_dim(quarters, quarter ^ m, 0, keepdims=False), 2 * m, devices)
        for m in (1, 2, 3)
    ]
    for part in parts:
        total = total + part
    mask = 8
    while mask < devices:
        total = total + swap(total, mask, devices)
        mask *= 2
    mine = [total] + [swap(total, 2 * m, devices) for m in (1, 2, 3)]
    other = [swap(piece, 1, devices) for piece in mine]

    def kernel(*refs):
        factor_kernel(1.0 / (slab * devices), refs[0], refs[1:9], *refs[9:])

    basis, factor = pl.pallas_call(
        kernel,
        out_shape=(
            jax.ShapeDtypeStruct((modes, slab), jnp.bfloat16),
            jax.ShapeDtypeStruct((runs, runs), jnp.float32),
        ),
        in_specs=[smem] + [vmem] * 10,
        out_specs=(vmem, pl.BlockSpec(memory_space=pl.ANY)),
        scratch_shapes=[
            pltpu.VMEM((packed, LANES), jnp.float32),
            pltpu.VMEM((len(upper_pairs(blocks)) * BLOCK, LANES), jnp.float32),
            pltpu.VMEM((runs, runs), jnp.float32),
            pltpu.VMEM((runs, runs), jnp.float32),
            pltpu.VMEM((modes, runs), jnp.float32),
            pltpu.SemaphoreType.DMA((blocks,)),
        ],
        compiler_params=pltpu.CompilerParams(vmem_limit_bytes=32 * 2**20),
    )(jnp.stack([half, quarter]).astype(jnp.int32), *mine, *other, design, anomaly)
    return (basis.reshape(modes, 1, slab), factor)


def solution(mesh):
    in_specs = (P("cells", "rep", None), P("rep", "cells"), P())
    out_specs = (P(None, "rep", "cells"), P())
    return jax.shard_map(shards, mesh=mesh, in_specs=in_specs, out_specs=out_specs, check_vma=False)
```

```python
import functools

import jax
import jax.numpy as jnp
from jax import lax
from jax.experimental import pallas as pl
from jax.experimental.pallas import tpu as pltpu
from jax.sharding import PartitionSpec as P

BLOCK = 128
HALF = BLOCK // 2
LANES = 128
AXES = ("cells", "rep")
HIGH = lax.Precision.HIGHEST
NARROW = (((1,), (0,)), ((), ()))
FIRST = (((0,), (0,)), ((), ()))
LAST = (((1,), (1,)), ((), ()))


def dot(a, b, dims=NARROW):
    return lax.dot_general(a, b, dims, precision=HIGH, preferred_element_type=jnp.float32)


def upper_pairs(count):
    return [(i, j) for i in range(count) for j in range(i, count)]


def packing(count):
    places, tails, at = {}, [], 0
    for i, j in upper_pairs(count):
        places[i, j] = at
        at += HALF if i == j else BLOCK
    for _ in range(count // 2):
        tails.append(at)
        at += HALF
    return places, tails, at


def factor_half(rows, shift, work):
    tile = (8, LANES)
    sub = lax.broadcasted_iota(jnp.int32, tile, 0)
    both = jnp.where(own_lanes(shift), rows, unit_rows(HALF - shift))
    count = HALF // 8
    strips = [both[8 * j : 8 * j + 8, :] for j in range(count)]

    def spread_row(value, at):
        return jnp.broadcast_to(value[at : at + 1, :], tile)

    def spread_column(value, at):
        return jnp.broadcast_to(value[:, shift + at : shift + at + 1], tile)

    ahead = [spread_column(strips[0], t) for t in range(8)]
    for m in range(count):
        columns, near = ahead, {}
        close = range(m + 1, min(m + 1 + 8, count))
        for j in close:
            for t in range(8):
                near[j, t] = spread_column(strips[j], 8 * m + t)
        if m + 1 < count:
            ahead = [spread_column(strips[m + 1], 8 * m + 8 + t) for t in range(8)]
        corner = {(t, u): spread_row(columns[u], t) for t in range(8) for u in range(t, 8)}
        rows_left = [spread_row(strips[m], t) for t in range(8)]
        lines = []
        for t in range(8):
            root = lax.rsqrt(corner[t, t])
            line = {u: corner[t, u] * root for u in range(t + 1, 8)}
            for u in range(t + 1, 8):
                for v in range(u, 8):
                    corner[u, v] = corner[u, v] - line[u] * line[v]
            row = rows_left[t] * root
            lines.append(row)
            for u in range(t + 1, 8):
                rows_left[u] = rows_left[u] - line[u] * row
            for j in close:
                column = near[j, t] * root
                for u in range(t + 1, 8):
                    near[j, u] = near[j, u] - column * line[u]
                strips[j] = strips[j] - column * row
                if j == m + 1:
                    ahead = [ahead[u] - column * spread_row(column, u) for u in range(8)]
        done = lines[0]
        for t in range(1, 8):
            done = jnp.where(sub == t, lines[t], done)
        strips[m] = done
        for _ in range(-(-len(work) // (count - m))):
            work.pop(0)()
    return jnp.concatenate(strips, axis=0)


def lane_index():
    return lax.broadcasted_iota(jnp.int32, (HALF, LANES), 1)


def row_index():
    return lax.broadcasted_iota(jnp.int32, (HALF, LANES), 0)


def own_lanes(shift):
    return lane_index() < HALF if shift == 0 else lane_index() >= HALF


def unit_rows(shift):
    return (lane_index() == row_index() + shift).astype(jnp.float32)


def pack_kernel(partners, waited, place_ref, field_ref, *refs):
    piece_refs = refs[waited:]
    slab = piece_refs[0].shape[1]
    for partner, piece_ref in zip(partners, piece_refs):
        start = lax.bitwise_xor(place_ref[0], partner) * slab
        piece_ref[...] = field_ref[:, pl.ds(pl.multiple_of(start, LANES), slab)]


def gram_kernel(place_ref, *refs):
    *piece_refs, base_ref, anomaly_ref, gram_ref = refs
    count = anomaly_ref.shape[0] // BLOCK
    base = base_ref[...].astype(jnp.float32)
    for partner, piece_ref in enumerate(piece_refs):
        size = piece_ref.shape[0]
        start = lax.bitwise_xor(place_ref[0], partner) * size if len(piece_refs) > 1 else 0
        anomaly_ref[pl.ds(pl.multiple_of(start, size), size), :] = (
            piece_ref[...].astype(jnp.float32) - base
        ).astype(jnp.bfloat16)
    places, tails, _ = packing(count)
    kept = None
    for i in range(count):
        if i % 2 == 0:
            rows = anomaly_ref[pl.ds(i * BLOCK, 2 * BLOCK), :]
            rest = anomaly_ref[pl.ds(i * BLOCK, (count - i) * BLOCK), :]
            wide = lax.dot_general(rows, rest, LAST, preferred_element_type=jnp.float32)
        part = wide[:BLOCK, :] if i % 2 == 0 else wide[BLOCK:, BLOCK:]
        gram_ref[pl.ds(places[i, i], HALF), :] = part[:HALF, :BLOCK]
        for j in range(i + 1, count):
            at = (j - i) * BLOCK
            gram_ref[pl.ds(places[i, j], BLOCK), :] = part[:, at : at + BLOCK]
        corner = part[HALF:, HALF:BLOCK]
        if i % 2 == 0:
            kept = corner
        else:
            gram_ref[pl.ds(tails[i // 2], HALF), :] = jnp.concatenate([kept, corner], axis=1)


def factor_kernel(
    scale,
    place_ref,
    piece_refs,
    design_ref,
    anomaly_ref,
    basis_ref,
    out_ref,
    packed_ref,
    gram_ref,
    inv_ref,
    factor_ref,
    mix_ref,
    sems,
):
    count = factor_ref.shape[0] // BLOCK
    slots, size = len(piece_refs) // 2, piece_refs[0].shape[0]
    half, quarter = place_ref[0], place_ref[1]
    for slot in range(slots):
        piece = lax.bitwise_xor(quarter, slot)
        for side, ref in ((half, piece_refs[slot]), (1 - half, piece_refs[slots + slot])):
            start = pl.multiple_of((side * slots + piece) * size, 8)
            packed_ref[pl.ds(start, size), :] = ref[...] * scale
    places, tails, _ = packing(count)
    where = {pair: at for at, pair in enumerate(upper_pairs(count))}
    for (i, j), at in where.items():
        size = HALF if i == j else BLOCK
        gram_ref[pl.ds(at * BLOCK, size), :] = packed_ref[pl.ds(places[i, j], size), :]
        if i == j:
            corner = packed_ref[pl.ds(tails[i // 2], HALF), :]
            if i % 2 == 0:
                corner = jnp.concatenate([corner[:, :HALF], corner[:, :HALF]], axis=1)
            gram_ref[pl.ds(at * BLOCK + HALF, HALF), :] = corner
    zero = jnp.zeros((HALF, LANES), jnp.float32)

    def gram_at(i, j, side=None):
        start = where[i, j] * BLOCK
        return pl.ds(start, BLOCK) if side is None else pl.ds(start + side * HALF, HALF)

    def span(i, side=None):
        return pl.ds(i * BLOCK, BLOCK) if side is None else pl.ds(i * BLOCK + side * HALF, HALF)

    def apply(solved, side, rows):
        return dot(solved, jnp.concatenate([zero, rows] if side == 0 else [rows, zero], axis=0))

    def row_factor(k, side, solved, j):
        def run():
            factor_ref[span(k, side), span(j)] = apply(solved, side, gram_ref[gram_at(k, j, side), :])

        return run

    def row_inverse(k, side, solved, j):
        def run():
            if j < k:
                rows = inv_ref[span(k, side), span(j)]
            elif side == 0:
                rows = unit_rows(0)
            else:
                rows = inv_ref[span(k, 1), span(k)] + unit_rows(HALF)
            inv_ref[span(k, side), span(j)] = apply(solved, side, rows)

        return run

    def lower_gram(k, first, j):
        def run():
            part = dot(first, factor_ref[span(k, 0), span(j)], FIRST)[HALF:, :]
            gram_ref[gram_at(k, j, 1), :] = gram_ref[gram_at(k, j, 1), :] - part

        return run

    def lower_inverse(k, first, j):
        def run():
            part = dot(first, inv_ref[span(k, 0), span(j)], FIRST)[HALF:, :]
            old = inv_ref[span(k, 1), span(j)] if j < k else 0.0
            inv_ref[span(k, 1), span(j)] = old - part

        return run

    def next_gram(k, side):
        def run():
            rows = factor_ref[span(k, side), span(k + 1)]
            at = gram_at(k + 1, k + 1)
            gram_ref[at, :] = gram_ref[at, :] - dot(rows, rows, FIRST)

        return run

    def later_gram(k, i, j):
        def run():
            part = dot(factor_ref[span(k), span(i)], factor_ref[span(k), span(j)], FIRST)
            gram_ref[gram_at(i, j), :] = gram_ref[gram_at(i, j), :] - part

        return run

    def later_inverse(k, i, j):
        def run():
            part = dot(factor_ref[span(k), span(i)], inv_ref[span(k), span(j)], FIRST)
            old = inv_ref[span(i), span(j)] if j < k else 0.0
            inv_ref[span(i), span(j)] = old - part

        return run

    def mix(k, j):
        def run():
            part = dot(design_ref[:, span(k)], inv_ref[span(k), span(j)])
            mix_ref[:, span(j)] = part if j == k else mix_ref[:, span(j)] + part

        return run

    def send(k):
        return pltpu.make_async_copy(
            factor_ref.at[span(k), :], out_ref.at[span(k), :], sems.at[k]
        )

    work = []
    for k in range(count):
        for j in range(k):
            factor_ref[span(k), span(j)] = jnp.zeros((BLOCK, BLOCK), jnp.float32)
        solved = factor_half(gram_ref[gram_at(k, k, 0), :], 0, work)
        first = apply(solved, 0, gram_ref[gram_at(k, k, 0), :])
        lower = gram_ref[gram_at(k, k, 1), :] - dot(first, first, FIRST)[HALF:, :]
        first = jnp.where(
            own_lanes(0), jnp.where(lane_index() >= row_index(), solved, 0.0), first
        )
        factor_ref[span(k, 0), span(k)] = first
        for j in range(k + 1, count):
            work += [row_factor(k, 0, solved, j), lower_gram(k, first, j)]
            if j == k + 1:
                work.append(next_gram(k, 0))
        for j in range(k + 1):
            work += [row_inverse(k, 0, solved, j), lower_inverse(k, first, j)]
        solved = factor_half(lower, HALF, work)
        factor_ref[span(k, 1), span(k)] = jnp.where(
            lane_index() >= row_index() + HALF, solved, 0.0
        )
        if k + 1 < count:
            row_factor(k, 1, solved, k + 1)()
            next_gram(k, 1)()
        for j in range(k + 2, count):
            work.append(row_factor(k, 1, solved, j))
        work.append(send(k).start)
        for i in range(k + 1, count):
            work += [later_gram(k, i, j) for j in range(i, count) if (i, j) != (k + 1, k + 1)]
        work += [row_inverse(k, 1, solved, j) for j in range(k + 1)]
        for i in range(k + 1, count):
            work += [later_inverse(k, i, j) for j in range(k + 1)]
        work += [mix(k, j) for j in range(k + 1)]
    while work:
        work.pop(0)()
    basis_ref[...] = lax.dot_general(
        mix_ref[...].astype(jnp.bfloat16),
        anomaly_ref[...],
        NARROW,
        preferred_element_type=jnp.float32,
    ).astype(jnp.bfloat16)
    for k in range(count):
        send(k).wait()


def swap(value, mask, devices):
    return lax.ppermute(value, AXES, [(i, i ^ mask) for i in range(devices)])


def shards(snapshots, base_field, design):
    n_cells, n_rep = lax.axis_size("cells"), lax.axis_size("rep")
    devices = n_cells * n_rep
    local_runs = snapshots.shape[0]
    runs, modes = design.shape
    slab = base_field.shape[1]
    blocks = runs // BLOCK
    packed = packing(blocks)[2]
    vmem = pl.BlockSpec(memory_space=pltpu.VMEM)
    smem = pl.BlockSpec(memory_space=pltpu.SMEM)
    column = lax.axis_index("cells").astype(jnp.int32).reshape(1)
    if n_cells == 8 and local_runs % 16 == 0:
        field = snapshots.reshape(local_runs, n_cells * slab)
        pieces = {}
        for partners, after in (((4, 5, 3, 0), ()), ((6, 7, 2, 1), (3,))):
            packed_pieces = pl.pallas_call(
                functools.partial(pack_kernel, partners, len(after)),
                out_shape=[jax.ShapeDtypeStruct((local_runs, slab), jnp.bfloat16)] * len(partners),
                in_specs=[smem, vmem] + [pl.BlockSpec(memory_space=pl.ANY)] * len(after),
                out_specs=[vmem] * len(partners),
                compiler_params=pltpu.CompilerParams(vmem_limit_bytes=16 * 2**20),
            )(column, field, *[pieces[m] for m in after])
            for m, piece in zip(partners, packed_pieces):
                route = [(i, i ^ m) for i in range(n_cells)]
                pieces[m] = lax.ppermute(piece, "cells", route) if m else piece
        panel = [pieces[m] for m in range(n_cells)]
    else:
        slabs = snapshots.reshape(local_runs, n_cells, slab).transpose(1, 0, 2)
        moved = lax.all_to_all(slabs, "cells", split_axis=0, concat_axis=0, tiled=True)
        panel = [moved.reshape(runs, slab)]
    anomaly, gram = pl.pallas_call(
        gram_kernel,
        out_shape=(
            jax.ShapeDtypeStruct((runs, slab), jnp.bfloat16),
            jax.ShapeDtypeStruct((packed, LANES), jnp.float32),
        ),
        in_specs=[smem] + [vmem] * (len(panel) + 1),
        out_specs=(vmem, vmem),
        compiler_params=pltpu.CompilerParams(vmem_limit_bytes=32 * 2**20),
    )(column, *panel, base_field)

    me = lax.axis_index("cells") * n_rep + lax.axis_index("rep")
    half, quarter = me % 2, (me // 2) % 4
    halves = gram.reshape(2, packed // 2, LANES)
    got = swap(lax.dynamic_index_in_dim(halves, 1 - half, 0, keepdims=False), 1, devices)
    own = lax.dynamic_index_in_dim(halves, half, 0, keepdims=False) + got
    quarters = own.reshape(4, packed // 8, LANES)
    total = lax.dynamic_index_in_dim(quarters, quarter, 0, keepdims=False)
    parts = [
        swap(lax.dynamic_index_in_dim(quarters, quarter ^ m, 0, keepdims=False), 2 * m, devices)
        for m in (1, 2, 3)
    ]
    for part in parts:
        total = total + part
    mask = 8
    while mask < devices:
        total = total + swap(total, mask, devices)
        mask *= 2
    mine = [total] + [swap(total, 2 * m, devices) for m in (1, 2, 3)]
    other = [swap(piece, 1, devices) for piece in mine]

    def kernel(*refs):
        factor_kernel(1.0 / (slab * devices), refs[0], refs[1:9], *refs[9:])

    basis, factor = pl.pallas_call(
        kernel,
        out_shape=(
            jax.ShapeDtypeStruct((modes, slab), jnp.bfloat16),
            jax.ShapeDtypeStruct((runs, runs), jnp.float32),
        ),
        in_specs=[smem] + [vmem] * 10,
        out_specs=(vmem, pl.BlockSpec(memory_space=pl.ANY)),
        scratch_shapes=[
            pltpu.VMEM((packed, LANES), jnp.float32),
            pltpu.VMEM((len(upper_pairs(blocks)) * BLOCK, LANES), jnp.float32),
            pltpu.VMEM((runs, runs), jnp.float32),
            pltpu.VMEM((runs, runs), jnp.float32),
            pltpu.VMEM((modes, runs), jnp.float32),
            pltpu.SemaphoreType.DMA((blocks,)),
        ],
        compiler_params=pltpu.CompilerParams(vmem_limit_bytes=32 * 2**20),
    )(jnp.stack([half, quarter]).astype(jnp.int32), *mine, *other, design.T, anomaly)
    return (basis.reshape(modes, 1, slab), factor)


def solution(mesh):
    in_specs = (P("cells", "rep", None), P("rep", "cells"), P())
    out_specs = (P(None, "rep", "cells"), P())
    return jax.shard_map(shards, mesh=mesh, in_specs=in_specs, out_specs=out_specs, check_vma=False)
```
